256 devices in a mesh: gx: 4 (over z_lo), gy: 4 (over z_hi, core), gz: 16 (over y, x).
Axes of the slice: x: 4, y: 4, z: 8 (z_hi: 2, z_lo: 4; z = z_hi * 4 + z_lo), core: 2. Of those that a mesh axis runs over, the one named last changes fastest.
Arguments:
- features: bfloat16 [262144, 128], P(('gx', 'gy', 'gz')), may hold values from -6 to 6
- up_weight: bfloat16 [128, 128], replicated, may hold values from -0.5 to 0.5
- radial_weight: bfloat16 [8, 384], replicated, may hold values from -2 to 2
- out_weight: bfloat16 [384, 128], replicated, may hold values from -0.3125 to 0.3125
- read_weight: float32 [4, 128], replicated, may hold values from -0.5 to 0.5
- ghost_rows: int32 [8, 8, 32, 32], P('gx', 'gy', 'gz'), may hold values from 0 to 1023, as said below
- senders: int32 [32, 262144], P(None, ('gx', 'gy', 'gz')), may hold values from 0 to 3071, as said below
- live: int32 [32, 262144], P(None, ('gx', 'gy', 'gz')), may hold values from 0 to 1, as said below
- harmonics: bfloat16 [9, 32, 262144], P(None, None, ('gx', 'gy', 'gz')), may hold values from -6 to 6
- radial: bfloat16 [8, 32, 262144], P(None, None, ('gx', 'gy', 'gz')), may hold values from -6 to 6
- species: int32 [262144], P(('gx', 'gy', 'gz')), may hold values from 0 to 3
- cotangent: float32 [262144], P(('gx', 'gy', 'gz')), may hold values from -6 to 6
Outputs:
- energy: float32 [262144], P(('gx', 'gy', 'gz'))
- feature_grad: float32 [262144, 128], P(('gx', 'gy', 'gz'))
- up_grad: float32 [128, 128], replicated
- radial_grad: float32 [8, 384], replicated
- out_grad: float32 [384, 128], replicated
- read_grad: float32 [4, 128], replicated
The draws below stay inside these ranges and needn't reach their ends.
Inputs may be any that keep to these rules, and one draw needn't show every extreme that they name: `ghost_rows`: every entry is a local atom row of the owning device; the 256 entries of one device are distinct. `senders`: an entry below 1024 is a local atom row of the same device; an entry v of 1024 or more is window row v - 1024, always in a cell (p, q, r) with p, q or r equal to 0 or 3. In each atom's column the live slots come first; every atom has 16 to 32 of them, and local atom 0 of every device has all 32.
All inputs are finite; a program needn't handle non-finite values.
Results may differ from the reference program's by a relative error of at most 0.0072.
Values may be sent and summed in bfloat16 or wider, within the bound.
A program may use at most 128 MiB of HBM per device.

```python
import math
import jax
import jax.numpy as jnp
import numpy as np
from jax import lax

C = 128
NB = 8
S = 4
K = 32
A = 1024
G = 32
ATOMS = 262144
N_GX = 4
N_GY = 4
N_GZ = 16


OUTER_CELLS = np.array([[p, q, r] for p in range(4) for q in range(4) for r in range(4) if min(p, q, r) == 0 or max(p, q, r) == 3], dtype=np.int32)


def pick_rows(single):
    order_key, roll_key = jax.random.split(single)
    order = jax.random.permutation(order_key, A - 1)[:8 * G - 1]
    row = jnp.concatenate([jnp.full((1,), A - 1, jnp.int32), order.astype(jnp.int32)])
    return jnp.roll(row, jax.random.randint(roll_key, (), 0, 8 * G))


def draw_ghost_rows(key, part):
    key = jax.random.fold_in(key, 11)
    device_keys = jax.random.split(key, N_GX * N_GY * N_GZ)
    chosen = jax.vmap(pick_rows)(device_keys).reshape(N_GX, N_GY, N_GZ, 2, 2, 2, G)
    return jnp.transpose(chosen, (0, 3, 1, 4, 2, 5, 6)).reshape(2 * N_GX, 2 * N_GY, 2 * N_GZ, G).astype(jnp.int32)


def draw_senders(key, part):
    key = jax.random.fold_in(key, 23)
    key_fill, key_cell, key_slot, key_local, key_kind = jax.random.split(key, 5)
    tile_fill = jax.random.randint(key_fill, (2 * N_GX, 2 * N_GY, 2 * N_GZ), max(1, G // 2), G + 1).at[0, 0, 0].set(G).at[2, 2, 2].set(G)
    device = jnp.arange(ATOMS, dtype=jnp.int32) // A
    coord_x = device // (N_GY * N_GZ)
    coord_y = device // N_GZ % N_GY
    coord_z = device % N_GZ
    picked = jnp.asarray(OUTER_CELLS)[jax.random.randint(key_cell, (K, ATOMS), 0, OUTER_CELLS.shape[0])]
    cell_p = picked[..., 0]
    cell_q = picked[..., 1]
    cell_r = picked[..., 2]
    global_x = (2 * coord_x[None, :] - 1 + cell_p) % (2 * N_GX)
    global_y = (2 * coord_y[None, :] - 1 + cell_q) % (2 * N_GY)
    global_z = (2 * coord_z[None, :] - 1 + cell_r) % (2 * N_GZ)
    cell_fill = tile_fill[global_x, global_y, global_z]
    slot_row = jax.random.randint(key_slot, (K, ATOMS), 0, 4096) * cell_fill // 4096
    ghost_value = A + ((cell_p * 4 + cell_q) * 4 + cell_r) * G + slot_row
    local_value = jax.random.randint(key_local, (K, ATOMS), 0, A)
    remote = jax.random.randint(key_kind, (K, ATOMS), 0, 20) < 7
    chosen = jnp.where(remote, ghost_value, local_value)
    return chosen.at[0, 0].set(A + 64 * G - 1).astype(jnp.int32)


def draw_live(key, part):
    key = jax.random.fold_in(key, 37)
    counts = jax.random.randint(key, (ATOMS,), max(1, K // 2), K + 1)
    leading = jnp.arange(ATOMS, dtype=jnp.int32) % A == 0
    counts = jnp.where(leading, K, counts)
    return (jnp.arange(K, dtype=jnp.int32)[:, None] < counts[None, :]).astype(jnp.int32)


def touch_ends(entries, key, low, largest):
    shape = entries.shape
    place = [jax.random.randint(jax.random.fold_in(key, axis), (), 0, shape[axis]) for axis in range(len(shape))]
    entries = entries.at[tuple(place)].set(low)
    longest = shape.index(max(shape))
    place[longest] = (place[longest] + 1) % shape[longest]
    return entries.at[tuple(place)].set(largest)


def steps_of(rng, dims, shards, low, largest):
    def one(position, blocks):
        draws = jax.random.uniform(jax.random.fold_in(jax.random.fold_in(rng, 6), position), (blocks,), jnp.float32, low / len(shards), largest / len(shards))
        return jnp.repeat(jnp.exp(draws), dims[position] // blocks).reshape((-1,) + (1,) * (len(dims) - position - 1))

    factor_of = one(*shards[0])
    for cut in shards[1:]:
        factor_of = factor_of * one(*cut)
    return factor_of


def bell_draw(key, dims, deviation, bound, cuts=(), held_as=jnp.bfloat16):
    values = deviation * jax.random.normal(key, dims, jnp.float32)
    if cuts:
        values = values * steps_of(key, dims, cuts, -0.22, 0.18)
    return jnp.clip(values, -bound, bound).astype(held_as)


def setup_inputs(seed: int = 0) -> dict:
    keys = jax.random.split(jax.random.key(seed), 13)
    features = bell_draw(keys[0], (ATOMS, C), 1.0, 6.0, ((0, 256),))
    up_weight = bell_draw(keys[1], (C, C), C ** -0.5, 0.5)
    radial_weight = bell_draw(keys[2], (NB, 3 * C), NB ** -0.5, 2.0)
    out_weight = bell_draw(keys[3], (3 * C, C), (3 * C) ** -0.5, 0.3125)
    read_weight = bell_draw(keys[4], (S, C), C ** -0.5, 0.5, (), jnp.float32)
    ghost_rows = draw_ghost_rows(jax.random.fold_in(keys[12], 71), 0)
    senders = draw_senders(jax.random.fold_in(keys[12], 71), 0)
    live = draw_live(jax.random.fold_in(keys[12], 71), 0)
    harmonics = bell_draw(keys[8], (9, K, ATOMS), 1.0, 6.0, ((2, 256),))
    radial = bell_draw(keys[9], (NB, K, ATOMS), 1.0, 6.0, ((2, 256),))
    species = touch_ends(jax.random.randint(keys[10], (ATOMS,), 0, S), jax.random.fold_in(keys[10], 1), 0, S - 1).astype(jnp.int32)
    cotangent = bell_draw(keys[11], (ATOMS,), 1.0, 6.0, ((0, 256),), jnp.float32)
    return {"features": features, "up_weight": up_weight, "radial_weight": radial_weight, "out_weight": out_weight, "read_weight": read_weight, "ghost_rows": ghost_rows, "senders": senders, "live": live, "harmonics": harmonics, "radial": radial, "species": species, "cotangent": cotangent}


DEGREE_OF = np.array([0, 1, 1, 1, 2, 2, 2, 2, 2])
HIGHEST = lax.Precision.HIGHEST

def atom_block(lookup, send_rows, live_rows, harm_rows, radial_rows, species_rows, cot_rows, feature_rows, radial_weight, out_weight, read_weight):
    channels = lookup.shape[1]
    norm_factor = 1.0 / math.sqrt(send_rows.shape[0])
    basis_count = radial_rows.shape[0]
    gathered = jnp.take(lookup, send_rows, axis=0)
    coupling = (live_rows.astype(jnp.float32)[None, None] * harm_rows.astype(jnp.float32)[:, None] * radial_rows.astype(jnp.float32)[None]).astype(jnp.bfloat16)
    mixed_sums = jnp.einsum('pnka,kac->pnac', coupling.astype(jnp.float32), gathered.astype(jnp.float32))
    radial_sel = jnp.transpose(radial_weight.astype(jnp.float32).reshape(basis_count, 3, channels)[:, DEGREE_OF], (1, 0, 2))
    amplitude = lax.optimization_barrier(jnp.sum(mixed_sums * radial_sel[:, :, None, :], axis=1)) * norm_factor
    invariants = jnp.concatenate([amplitude[0], lax.optimization_barrier(jnp.sum(amplitude[1:4] * amplitude[1:4], axis=0)), lax.optimization_barrier(jnp.sum(amplitude[4:] * amplitude[4:], axis=0))], axis=1).astype(jnp.bfloat16)
    updated = jnp.dot(invariants, out_weight, preferred_element_type=jnp.float32) + feature_rows.astype(jnp.float32)
    species_onehot = (species_rows[:, None] == jnp.arange(read_weight.shape[0], dtype=jnp.int32)[None, :]).astype(jnp.float32)
    readout = jnp.dot(species_onehot, read_weight, precision=HIGHEST)
    energy = lax.optimization_barrier(jnp.sum(updated * readout, axis=1))
    d_updated = cot_rows[:, None] * readout
    d_read = jnp.dot(species_onehot.T, cot_rows[:, None] * updated, precision=HIGHEST)
    d_rounded = d_updated.astype(jnp.bfloat16)
    d_out = jnp.dot(invariants.T, d_rounded, preferred_element_type=jnp.float32)
    d_inv = jnp.dot(d_rounded, out_weight.T, preferred_element_type=jnp.float32)
    d_amp = jnp.concatenate([d_inv[None, :, :channels], 2.0 * amplitude[1:4] * d_inv[None, :, channels:2 * channels], 2.0 * amplitude[4:] * d_inv[None, :, 2 * channels:]], axis=0) * norm_factor
    d_mixed = (d_amp[:, None] * radial_sel[:, :, None, :]).astype(jnp.bfloat16)
    d_sel = lax.optimization_barrier(jnp.sum(mixed_sums * d_amp[:, None], axis=2))
    d_radial = jnp.stack([d_sel[0], lax.optimization_barrier(jnp.sum(d_sel[1:4], axis=0)), lax.optimization_barrier(jnp.sum(d_sel[4:], axis=0))], axis=1).reshape(basis_count, 3 * channels)
    d_gathered = jnp.einsum('pnka,pnac->kac', coupling.astype(jnp.float32), d_mixed.astype(jnp.float32))
    return (energy, d_updated, d_read, d_out, d_radial, d_gathered)

def device_terms(lookup, senders, live, harmonics, radial, species, cotangent, features, radial_weight, out_weight, read_weight):
    atoms = senders.shape[1]
    channels = lookup.shape[1]
    block_len = min(512, atoms)

    def advance(block_no, carried):
        energy, d_res, d_lookup, d_read, d_out, d_radial = carried
        offset = block_no * block_len

        def across(source):
            return lax.dynamic_slice_in_dim(source, offset, block_len, source.ndim - 1)
        send_rows = across(senders)
        pieces = atom_block(lookup, send_rows, across(live), across(harmonics), across(radial), across(species), across(cotangent), lax.dynamic_slice_in_dim(features, offset, block_len, 0), radial_weight, out_weight, read_weight)
        e_part, res_part, read_part, out_part, radial_part, gathered_grad = pieces
        energy = lax.dynamic_update_slice_in_dim(energy, e_part, offset, 0)
        d_res = lax.dynamic_update_slice_in_dim(d_res, res_part, offset, 0)
        d_lookup = d_lookup.at[send_rows.reshape(-1)].add(gathered_grad.reshape(-1, channels))
        return (energy, d_res, d_lookup, d_read + read_part, d_out + out_part, d_radial + radial_part)
    initial = (jnp.zeros((atoms,), jnp.float32), jnp.zeros((atoms, channels), jnp.float32), jnp.zeros(lookup.shape, jnp.float32), jnp.zeros(read_weight.shape, jnp.float32), jnp.zeros(out_weight.shape, jnp.float32), jnp.zeros(radial_weight.shape, jnp.float32))
    return lax.fori_loop(0, atoms // block_len, advance, initial)

def wrap_pad(grid, axis):
    length = grid.shape[axis]
    return jnp.concatenate([lax.slice_in_dim(grid, length - 1, length, axis=axis), grid, lax.slice_in_dim(grid, 0, 1, axis=axis)], axis=axis)

def wrap_fold(grid, axis):
    length = grid.shape[axis]
    inner = lax.slice_in_dim(grid, 1, length - 1, axis=axis)
    span = length - 2
    first_row = lax.slice_in_dim(inner, 0, 1, axis=axis) + lax.slice_in_dim(grid, length - 1, length, axis=axis)
    last_row = lax.slice_in_dim(inner, span - 1, span, axis=axis) + lax.slice_in_dim(grid, 0, 1, axis=axis)
    return jnp.concatenate([first_row, lax.slice_in_dim(inner, 1, span - 1, axis=axis), last_row], axis=axis)

def reference(features, up_weight, radial_weight, out_weight, read_weight, ghost_rows, senders, live, harmonics, radial, species, cotangent):
    devices = N_GX * N_GY * N_GZ
    channels = features.shape[1]
    mixed_rows = jnp.dot(features, up_weight, preferred_element_type=jnp.float32).astype(jnp.bfloat16)
    octant_x = jnp.arange(2 * N_GX, dtype=jnp.int32) // 2
    octant_y = jnp.arange(2 * N_GY, dtype=jnp.int32) // 2
    octant_z = jnp.arange(2 * N_GZ, dtype=jnp.int32) // 2
    owner_dev = (octant_x[:, None, None] * N_GY + octant_y[None, :, None]) * N_GZ + octant_z[None, None, :]
    atom_of_tile = (owner_dev[..., None] * A + ghost_rows).reshape(-1).astype(jnp.int32)
    tiles = jnp.take(mixed_rows, atom_of_tile, axis=0).reshape(2 * N_GX, 2 * N_GY, 2 * N_GZ, G, channels)
    padded = wrap_pad(wrap_pad(wrap_pad(tiles, 0), 1), 2)

    def visit(device, carried):
        grid_grad, energy_all, own_grad, res_grad, d_read, d_out, d_radial = carried
        device = jnp.asarray(device).astype(jnp.int32)
        coord_x = device // (N_GY * N_GZ)
        coord_y = device // N_GZ % N_GY
        coord_z = device % N_GZ
        zero_idx = jnp.zeros((), jnp.int32)
        corner = (2 * coord_x, 2 * coord_y, 2 * coord_z, zero_idx, zero_idx)
        window = lax.dynamic_slice(padded, corner, (4, 4, 4, G, channels))
        first_atom = device * A
        lookup = jnp.concatenate([lax.dynamic_slice_in_dim(mixed_rows, first_atom, A, 0), window.reshape(64 * G, channels)], axis=0)

        def own_part(source):
            return lax.dynamic_slice_in_dim(source, first_atom, A, source.ndim - 1)
        results = device_terms(lookup, own_part(senders), own_part(live), own_part(harmonics), own_part(radial), own_part(species), own_part(cotangent), lax.dynamic_slice_in_dim(features, first_atom, A, 0), radial_weight, out_weight, read_weight)
        energy, d_res, d_lookup, read_part, out_part, radial_part = results
        grid_grad = lax.dynamic_update_slice(grid_grad, lax.dynamic_slice(grid_grad, corner, (4, 4, 4, G, channels)) + d_lookup[A:].reshape(4, 4, 4, G, channels), corner)
        energy_all = lax.dynamic_update_slice_in_dim(energy_all, energy, first_atom, 0)
        own_grad = lax.dynamic_update_slice_in_dim(own_grad, d_lookup[:A], first_atom, 0)
        res_grad = lax.dynamic_update_slice_in_dim(res_grad, d_res, first_atom, 0)
        return (grid_grad, energy_all, own_grad, res_grad, d_read + read_part, d_out + out_part, d_radial + radial_part)
    initial = (jnp.zeros(padded.shape, jnp.float32), jnp.zeros((ATOMS,), jnp.float32), jnp.zeros((ATOMS, channels), jnp.float32), jnp.zeros((ATOMS, channels), jnp.float32), jnp.zeros(read_weight.shape, jnp.float32), jnp.zeros(out_weight.shape, jnp.float32), jnp.zeros(radial_weight.shape, jnp.float32))
    grid_grad, energy_all, own_grad, res_grad, d_read, d_out, d_radial = lax.fori_loop(0, devices, visit, initial)
    d_tiles = wrap_fold(wrap_fold(wrap_fold(grid_grad, 0), 1), 2)
    d_mixed_rows = own_grad.at[atom_of_tile].add(d_tiles.reshape(-1, channels))
    up_wide = up_weight.astype(jnp.float32)
    feature_grad = jnp.dot(d_mixed_rows, up_wide.T, precision=HIGHEST) + res_grad
    factor = 1.0 / math.sqrt(ATOMS)
    up_grad = jnp.dot(features.astype(jnp.float32).T, d_mixed_rows, precision=HIGHEST) * factor
    return (energy_all, feature_grad, up_grad, d_radial * factor, d_out * factor, d_read * factor)
```

```python
import functools
import math

import jax
import jax.numpy as jnp
import numpy as np
from jax import lax
from jax.experimental import pallas as pl
from jax.experimental.pallas import tpu as pltpu
from jax.sharding import PartitionSpec as P

C = 128
LANES = 128
SLOTS = 32
ATOMS = 1024
BASIS = 8
PARTS = 9
WINDOW = 2048
TABLE = ATOMS + WINDOW
HALF = TABLE // 2
PER = ATOMS // LANES
EDGES = PER * SLOTS
BATCH = 4
DEGREE = (0, 1, 1, 1, 2, 2, 2, 2, 2)
F32 = jnp.float32
BF16 = jnp.bfloat16

NT = (((1,), (1,)), ((), ()))
TN = (((0,), (0,)), ((), ()))
NN = (((1,), (0,)), ((), ()))


def mm(a, b, dims):
    return lax.dot_general(a, b, dims, preferred_element_type=F32)


def turned(block):
    stacked = jnp.concatenate(
        [block[:, q * LANES : (q + 1) * LANES] for q in range(PER)], axis=0
    )
    return jnp.swapaxes(stacked, 0, 1)


def local_kernel(
    features, window, up, radial_w, out_w, read_w, senders, live, harm, radial, species, cot,
    energy_ref, d_upd_ref, d_own_ref, d_win_ref, grads_ref,
    table, low, high, half, y_t, r_t, w_ref, onehot, lhs, mixed, d_inv, inv, acc, gath, back, d_mix, rad_acc,
):
    up_v = up[...]
    def fill_table(source, count, first):
        part = mm(up_v, source, (((0,), (1,)), ((), ()))).astype(BF16)
        return part
    own = fill_table(features[...], ATOMS, 0)
    win = fill_table(window[...], WINDOW, ATOMS)
    table[0:C, 0:ATOMS] = own
    table[0:C, ATOMS:HALF] = win[:, 0 : HALF - ATOMS]
    table[C : 2 * C, :] = win[:, HALF - ATOMS :]

    send = turned(senders[...].astype(F32))
    second = (send >= HALF).astype(F32)
    within = send - second * HALF
    tens = jnp.floor(within * (1.0 / 16))
    half[...] = second
    high[...] = tens
    low[...] = within - tens * 16
    alive = live[...].astype(F32)
    for m in range(PARTS):
        y_t[m] = turned(harm[m].astype(F32) * alive)
    for n in range(BASIS):
        r_t[n] = turned(radial[n].astype(F32))

    for n in range(BASIS):
        for l in range(3):
            w_ref[n * 3 + l] = jnp.broadcast_to(
                radial_w[n : n + 1, l * C : (l + 1) * C].astype(F32), (8, C)
            )

    for q in range(PER):
        kind = jnp.swapaxes(jnp.broadcast_to(species[q : q + 1, :], (LANES, LANES)), 0, 1)
        weight = jnp.swapaxes(jnp.broadcast_to(cot[q : q + 1, :], (LANES, LANES)), 0, 1)
        readout = jnp.zeros((LANES, C), F32)
        for t in range(4):
            readout = jnp.where(kind == t, read_w[t : t + 1, :], readout)
        d_upd = weight * readout
        d_upd_ref[q * LANES : (q + 1) * LANES, :] = d_upd
        d_part = mm(d_upd.astype(BF16), out_w[...], NT)
        for l in range(3):
            d_inv[l, q * LANES : (q + 1) * LANES, :] = d_part[:, l * C : (l + 1) * C]

    acc[...] = jnp.zeros_like(acc)
    rad_acc[...] = jnp.zeros_like(rad_acc)

    sub16 = lax.broadcasted_iota(jnp.int32, (16, EDGES), 0)
    lane16 = lax.broadcasted_iota(jnp.int32, (16, EDGES), 1)
    owner = (sub16 & 7) == (lane16 >> 5)
    sub16f = sub16.astype(F32).astype(BF16)
    norm = 1.0 / math.sqrt(SLOTS)

    def step(i, carry):
        for g in range(BATCH):
            a = i * BATCH + g
            lo = jnp.broadcast_to(low[pl.ds(a, 1), :], (16, EDGES)).astype(BF16)
            hi = jnp.broadcast_to(high[pl.ds(a, 1), :], (16, EDGES)).astype(BF16)
            z = jnp.where(lo == sub16f, hi, jnp.full_like(hi, -1))
            for block in range(HALF // 16):
                onehot[block * 16 : block * 16 + 16, g * EDGES : (g + 1) * EDGES] = jnp.where(
                    z == block, jnp.ones_like(z), jnp.zeros_like(z)
                )
        for g in range(BATCH):
            a = i * BATCH + g
            cols = slice(g * EDGES, (g + 1) * EDGES)
            second = jnp.broadcast_to(half[pl.ds(a, 1), :], (C, EDGES)) > 0.5
            both = mm(table[...], onehot[:, cols], NN)
            gathered = jnp.where(second, both[C:], both[:C]).astype(BF16)
            r16 = []
            for j in range(BASIS // 2):
                r16.append(
                    jnp.concatenate(
                        [
                            jnp.broadcast_to(r_t[2 * j + k, pl.ds(a, 1), :], (8, EDGES))
                            for k in range(2)
                        ],
                        axis=0,
                    ).astype(BF16)
                )
            for m in range(PARTS):
                y16 = jnp.where(
                    owner, jnp.broadcast_to(y_t[m, pl.ds(a, 1), :], (16, EDGES)), 0.0
                ).astype(BF16)
                for j in range(BASIS // 2):
                    row = m * 64 + j * 16
                    lhs[g, row : row + 16, :] = y16 * r16[j]
            mixed[g] = mm(lhs[g], gathered, NT)
            amps = []
            for m in range(PARTS):
                total = None
                for n in range(BASIS):
                    term = mixed[g, m * 64 + n * 8 : m * 64 + n * 8 + 8, :] * w_ref[n * 3 + DEGREE[m]]
                    total = term if total is None else total + term
                amps.append(total * norm)
            inv1 = amps[1] * amps[1] + amps[2] * amps[2] + amps[3] * amps[3]
            inv2 = sum(amps[m] * amps[m] for m in range(5, 9)) + amps[4] * amps[4]
            for l, value in enumerate((amps[0], inv1, inv2)):
                inv[l, pl.ds(a, 8, stride=LANES), :] = value
            d_l = [d_inv[l, pl.ds(a, 8, stride=LANES), :] * norm for l in range(3)]
            d_amps = [d_l[0]]
            for m in range(1, PARTS):
                d_amps.append(2.0 * amps[m] * d_l[DEGREE[m]])
            for n in range(BASIS):
                for l in range(3):
                    total = None
                    for m in range(PARTS):
                        if DEGREE[m] != l:
                            continue
                        term = mixed[g, m * 64 + n * 8 : m * 64 + n * 8 + 8, :] * d_amps[m]
                        total = term if total is None else total + term
                    rad_acc[n * 3 + l] += total
            for m in range(PARTS):
                for j in range(BASIS // 2):
                    row = m * 64 + j * 16
                    d_mix[g, row : row + 16, :] = jnp.concatenate(
                        [d_amps[m] * w_ref[(2 * j + k) * 3 + DEGREE[m]] for k in range(2)], axis=0
                    ).astype(BF16)
            d_t = mm(d_mix[g], lhs[g], TN)
            back[0:C, cols] = jnp.where(second, 0.0, d_t).astype(BF16)
            back[C : 2 * C, cols] = jnp.where(second, d_t, 0.0).astype(BF16)
        acc[...] += mm(onehot[...], back[...], NT)
        return carry

    lax.fori_loop(0, LANES // BATCH, step, 0)

    d_out = jnp.zeros((3 * C, C), F32)
    read_rows = [jnp.zeros((1, C), F32) for _ in range(4)]
    for q in range(PER):
        rows = slice(q * LANES, (q + 1) * LANES)
        invariants = jnp.concatenate([inv[l, rows, :] for l in range(3)], axis=1).astype(BF16)
        updated = mm(invariants, out_w[...], NN) + features[rows, :].astype(F32)
        kind = jnp.swapaxes(jnp.broadcast_to(species[q : q + 1, :], (LANES, LANES)), 0, 1)
        weight = jnp.swapaxes(jnp.broadcast_to(cot[q : q + 1, :], (LANES, LANES)), 0, 1)
        readout = jnp.zeros((LANES, C), F32)
        for t in range(4):
            readout = jnp.where(kind == t, read_w[t : t + 1, :], readout)
            read_rows[t] = read_rows[t] + jnp.sum(
                jnp.where(kind == t, weight * updated, 0.0), axis=0, keepdims=True
            )
        energy_ref[q : q + 1, :] = jnp.sum(
            jnp.swapaxes(updated * readout, 0, 1), axis=0, keepdims=True
        )
        d_rounded = d_upd_ref[rows, :].astype(BF16)
        d_out = d_out + mm(invariants, d_rounded, TN)
    d_own = acc[0:ATOMS, 0:C]
    d_own_ref[...] = d_own
    d_win = jnp.concatenate([acc[ATOMS:HALF, 0:C], acc[:, C : 2 * C]], axis=0).astype(BF16)
    d_win_ref[...] = d_win
    up_sum = mm(features[...], d_own.astype(BF16), TN) + mm(window[...], d_win, TN)
    large = jnp.concatenate([up_sum, d_out], axis=0)
    blank = jnp.zeros((8, C), F32)
    for piece in range(16):
        if piece < 3:
            small = jnp.concatenate(
                [jnp.sum(rad_acc[n * 3 + piece], axis=0, keepdims=True) for n in range(BASIS)], axis=0
            )
        elif piece == 3:
            small = jnp.concatenate(read_rows + [jnp.zeros((4, C), F32)], axis=0)
        else:
            small = blank
        grads_ref[piece] = jnp.concatenate(
            [large[piece * 32 : piece * 32 + 32], small, blank], axis=0
        ).astype(BF16)


def local_terms(features, window, up, radial_w, out_w, read_w, senders, live, harm, radial, species, cot):
    vm = pl.BlockSpec(memory_space=pltpu.VMEM)
    return pl.pallas_call(
        local_kernel,
        out_shape=(
            jax.ShapeDtypeStruct((PER, LANES), F32),
            jax.ShapeDtypeStruct((ATOMS, C), F32),
            jax.ShapeDtypeStruct((ATOMS, C), F32),
            jax.ShapeDtypeStruct((WINDOW, C), BF16),
            jax.ShapeDtypeStruct((16, 48, C), BF16),
        ),
        in_specs=[vm] * 12,
        out_specs=(vm,) * 5,
        scratch_shapes=[
            pltpu.VMEM((2 * C, HALF), BF16),
            pltpu.VMEM((LANES, EDGES), F32),
            pltpu.VMEM((LANES, EDGES), F32),
            pltpu.VMEM((LANES, EDGES), F32),
            pltpu.VMEM((PARTS, LANES, EDGES), F32),
            pltpu.VMEM((BASIS, LANES, EDGES), F32),
            pltpu.VMEM((3 * BASIS, 8, C), F32),
            pltpu.VMEM((HALF, BATCH * EDGES), BF16),
            pltpu.VMEM((BATCH, PARTS * BASIS * 8, EDGES), BF16),
            pltpu.VMEM((BATCH, PARTS * BASIS * 8, C), F32),
            pltpu.VMEM((3, ATOMS, C), F32),
            pltpu.VMEM((3, ATOMS, C), F32),
            pltpu.VMEM((HALF, 2 * C), F32),
            pltpu.VMEM((8, 128), F32),
            pltpu.VMEM((2 * C, BATCH * EDGES), BF16),
            pltpu.VMEM((BATCH, PARTS * BASIS * 8, C), BF16),
            pltpu.VMEM((3 * BASIS, 8, C), F32),
        ],
        compiler_params=pltpu.CompilerParams(vmem_limit_bytes=48 * 1024 * 1024),
    )(features, window, up, radial_w, out_w, read_w, senders, live, harm, radial, species, cot)


AXES = ("gx", "gy", "gz")
MESH = pl.DeviceIdType.MESH
GHOST = 32
PIECES = 16
PIECE_ROWS = 48


def place():
    return {axis: lax.axis_index(axis) for axis in AXES}


def shifted(axis, by):
    me = place()
    me[axis] = lax.rem(me[axis] + by + lax.axis_size(axis), lax.axis_size(axis))
    return tuple(me[name] for name in AXES)


def remote(source, target, send, arrive, device):
    return pltpu.make_async_remote_copy(
        src_ref=source,
        dst_ref=target,
        send_sem=send,
        recv_sem=arrive,
        device_id=device,
        device_id_type=MESH,
    )


def column(row):
    return jnp.swapaxes(jnp.broadcast_to(row, (LANES, LANES)), 0, 1)


def spread_kernel(features, ghost, window, send, arrive):
    barrier = pltpu.get_barrier_semaphore()
    for axis in AXES:
        for by in (1, -1):
            pl.semaphore_signal(barrier, inc=1, device_id=shifted(axis, by), device_id_type=MESH)
    lane = lax.broadcasted_iota(jnp.int32, (LANES, LANES), 1)
    for h in range(2):
        rows = column(ghost[h : h + 1, :])
        hot = jnp.concatenate(
            [
                jnp.where(rows == lane + block * LANES, 1.0, 0.0).astype(BF16)
                for block in range(ATOMS // LANES)
            ],
            axis=1,
        )
        picked = mm(hot, features[...], NN).astype(BF16)
        for j in range(2):
            for k in range(2):
                first = (j * 2 + k) * GHOST
                window[1 + h, 1 + j, 1 + k] = picked[first : first + GHOST, :]
    pl.semaphore_wait(barrier, 6)
    inner = pl.ds(1, 2)
    plans = (
        ("gy", lambda at: window.at[inner, at, inner]),
        ("gx", lambda at: window.at[at, :, inner]),
        ("gz", lambda at: window.at[:, :, at]),
    )
    for number, (axis, view) in enumerate(plans):
        up = remote(
            view(2), view(0), send.at[2 * number], arrive.at[2 * number], shifted(axis, 1)
        )
        down = remote(
            view(1), view(3), send.at[2 * number + 1], arrive.at[2 * number + 1], shifted(axis, -1)
        )
        up.start()
        down.start()
        up.wait()
        down.wait()


def spread(features, ghost):
    vm = pl.BlockSpec(memory_space=pltpu.VMEM)
    return pl.pallas_call(
        spread_kernel,
        out_shape=jax.ShapeDtypeStruct((4, 4, 4, GHOST, C), BF16),
        in_specs=[vm] * 2,
        out_specs=vm,
        scratch_shapes=[pltpu.SemaphoreType.DMA((6,)), pltpu.SemaphoreType.DMA((6,))],
        compiler_params=pltpu.CompilerParams(
            collective_id=0, has_side_effects=True, vmem_limit_bytes=32 * 1024 * 1024
        ),
    )(features, ghost)


def plane_device(by):
    return shifted("gz", by)


def stack_device(by):
    me = place()
    wide = lax.axis_size("gy")
    count = lax.axis_size("gx") * wide
    other = lax.rem(me["gx"] * wide + me["gy"] + by, count)
    return (lax.div(other, wide), lax.rem(other, wide), me["gz"]), other


def finish_kernel(
    scale, d_win, grads, d_own, d_upd, ghost, up,
    feature_grad, up_grad, rad_grad, out_grad, read_grad,
    from_z, from_x, from_y, wide, narrow, first, second, third,
    near_send, near_arrive, send1, arrive1, send2, arrive2, send3, arrive3,
):
    me = place()
    k = me["gz"]
    s = me["gx"] * lax.axis_size("gy") + me["gy"]

    barrier = pltpu.get_barrier_semaphore()

    def greet(by, carry):
        pl.semaphore_signal(barrier, inc=1, device_id=plane_device(by), device_id_type=MESH)
        pl.semaphore_signal(barrier, inc=1, device_id=stack_device(by)[0], device_id_type=MESH)
        return carry

    lax.fori_loop(1, PIECES, greet, 0)
    pl.semaphore_wait(barrier, 2 * (PIECES - 1))

    def near(number, low_view, high_view, landing, axis):
        down = remote(
            low_view, landing.at[0], near_send.at[2 * number], near_arrive.at[2 * number],
            shifted(axis, -1),
        )
        above = remote(
            high_view, landing.at[1], near_send.at[2 * number + 1], near_arrive.at[2 * number + 1],
            shifted(axis, 1),
        )
        down.start()
        above.start()
        return down, above

    copies_z = near(0, d_win.at[:, :, 0], d_win.at[:, :, 3], from_z, "gz")

    def copy1(by):
        target = lax.rem(k + by, PIECES)
        return remote(
            grads.at[target], first.at[k], send1.at[target], arrive1.at[k], plane_device(by)
        )

    def copy2(by):
        device, other = stack_device(by)
        return remote(second.at[s], second.at[s], send2.at[other], arrive2.at[s], device)

    def copy3(by):
        target = lax.rem(k + by, PIECES)
        return remote(third.at[k], third.at[k], send3.at[target], arrive3.at[k], plane_device(by))

    def started(copy):
        def body(by, carry):
            copy(by).start()
            return carry

        lax.fori_loop(1, PIECES, body, 0)

    def settled(copy, slots, sems, mine):
        def body(by, carry):
            copy(by).wait_send()
            source = lax.rem(mine + by, PIECES)
            remote(
                slots.at[source], slots.at[source], sems.at[source], sems.at[source],
                plane_device(1),
            ).wait_recv()
            return carry

        lax.fori_loop(1, PIECES, body, 0)

    started(copy1)
    first[k] = grads[k]

    for copy in copies_z:
        copy.wait()
    wide[:, :, 0] = (d_win[:, :, 1].astype(F32) + from_z[1].astype(F32)).astype(BF16)
    wide[:, :, 1] = (d_win[:, :, 2].astype(F32) + from_z[0].astype(F32)).astype(BF16)
    copies_x = near(1, wide.at[0], wide.at[3], from_x, "gx")

    settled(copy1, first, arrive1, k)
    second[s] = sum_of(first)
    started(copy2)

    for copy in copies_x:
        copy.wait()
    narrow[0] = (wide[1].astype(F32) + from_x[1].astype(F32)).astype(BF16)
    narrow[1] = (wide[2].astype(F32) + from_x[0].astype(F32)).astype(BF16)
    copies_y = near(2, narrow.at[:, 0], narrow.at[:, 3], from_y, "gy")

    settled(copy2, second, arrive2, s)
    third[k] = sum_of(second)
    started(copy3)

    for copy in copies_y:
        copy.wait()
    atom = lax.broadcasted_iota(jnp.int32, (ATOMS, LANES), 0)
    total = d_own[...]
    for h in range(2):
        sides = (
            narrow[h, 1].astype(F32) + from_y[1, h].astype(F32),
            narrow[h, 2].astype(F32) + from_y[0, h].astype(F32),
        )
        folded = jnp.concatenate([side.reshape(2 * GHOST, C) for side in sides], axis=0).astype(BF16)
        hot = jnp.where(atom == ghost[h : h + 1, :], 1.0, 0.0).astype(BF16)
        total = total + mm(hot, folded, NN)
    feature_grad[...] = mm(total.astype(BF16), up[...], NT) + d_upd[...]

    settled(copy3, third, arrive3, k)
    for piece in range(4):
        up_grad[piece * 32 : piece * 32 + 32, :] = third[piece, 0:32].astype(F32) * scale
    for piece in range(12):
        out_grad[piece * 32 : piece * 32 + 32, :] = third[4 + piece, 0:32].astype(F32) * scale
    for l in range(3):
        rad_grad[:, l * C : (l + 1) * C] = third[l, 32:48].astype(F32)[0:8] * scale
    read_grad[...] = third[3, 32:48].astype(F32)[0:4] * scale


def sum_of(slots):
    total = slots[0].astype(F32)
    for piece in range(1, PIECES):
        total = total + slots[piece].astype(F32)
    return total.astype(BF16)


def finish(scale, d_win, grads, d_own, d_upd, ghost, up):
    vm = pl.BlockSpec(memory_space=pltpu.VMEM)
    sems = pltpu.SemaphoreType.DMA((PIECES,))
    return pl.pallas_call(
        functools.partial(finish_kernel, scale),
        out_shape=(
            jax.ShapeDtypeStruct((ATOMS, C), F32),
            jax.ShapeDtypeStruct((C, C), F32),
            jax.ShapeDtypeStruct((BASIS, 3 * C), F32),
            jax.ShapeDtypeStruct((3 * C, C), F32),
            jax.ShapeDtypeStruct((4, C), F32),
        ),
        in_specs=[vm] * 6,
        out_specs=(vm,) * 5,
        scratch_shapes=[
            pltpu.VMEM((2, 4, 4, GHOST, C), BF16),
            pltpu.VMEM((2, 4, 2, GHOST, C), BF16),
            pltpu.VMEM((2, 2, 2, GHOST, C), BF16),
            pltpu.VMEM((4, 4, 2, GHOST, C), BF16),
            pltpu.VMEM((2, 4, 2, GHOST, C), BF16),
            pltpu.VMEM((PIECES, PIECE_ROWS, C), BF16),
            pltpu.VMEM((PIECES, PIECE_ROWS, C), BF16),
            pltpu.VMEM((PIECES, PIECE_ROWS, C), BF16),
            pltpu.SemaphoreType.DMA((6,)),
            pltpu.SemaphoreType.DMA((6,)),
            sems, sems, sems, sems, sems, sems,
        ],
        compiler_params=pltpu.CompilerParams(
            collective_id=1, has_side_effects=True, vmem_limit_bytes=32 * 1024 * 1024
        ),
    )(d_win, grads, d_own, d_upd, ghost, up)


def per_device(
    features, up_weight, radial_weight, out_weight, read_weight,
    ghost_rows, senders, live, harmonics, radial, species, cotangent,
):
    ghost = ghost_rows.reshape(2, LANES)
    window = spread(features, ghost)
    energy, d_upd, d_own, d_win, grads = local_terms(
        features, window.reshape(WINDOW, C), up_weight, radial_weight, out_weight, read_weight,
        senders, live, harmonics, radial,
        species.reshape(PER, LANES), cotangent.reshape(PER, LANES),
    )
    scale = 1.0 / math.sqrt(ATOMS * lax.axis_size("gx") * lax.axis_size("gy") * lax.axis_size("gz"))
    feature_grad, up_grad, rad_grad, out_grad, read_grad = finish(
        scale, d_win.reshape(4, 4, 4, GHOST, C), grads, d_own, d_upd, ghost, up_weight
    )
    return energy.reshape(ATOMS), feature_grad, up_grad, rad_grad, out_grad, read_grad


def solution(mesh):
    whole = P(AXES)
    in_specs = (
        P(AXES, None), P(), P(), P(), P(),
        P("gx", "gy", "gz", None), P(None, AXES), P(None, AXES), P(None, None, AXES),
        P(None, None, AXES), whole, whole,
    )
    out_specs = (whole, P(AXES, None), P(), P(), P(), P())
    return jax.shard_map(
        per_device, mesh=mesh, in_specs=in_specs, out_specs=out_specs, check_vma=False
    )
```

```python
import functools
import math

import jax
import jax.numpy as jnp
import numpy as np
from jax import lax
from jax.experimental import pallas as pl
from jax.experimental.pallas import tpu as pltpu
from jax.sharding import PartitionSpec as P

C = 128
LANES = 128
SLOTS = 32
ATOMS = 1024
BASIS = 8
PARTS = 9
WINDOW = 2048
TABLE = ATOMS + WINDOW
HALF = TABLE // 2
PER = ATOMS // LANES
EDGES = PER * SLOTS
BATCH = 16
DEGREE = (0, 1, 1, 1, 2, 2, 2, 2, 2)
F32 = jnp.float32
BF16 = jnp.bfloat16

CHUNK = 256
NT = (((1,), (1,)), ((), ()))
TN = (((0,), (0,)), ((), ()))
NN = (((1,), (0,)), ((), ()))


def mm(a, b, dims):
    return lax.dot_general(a, b, dims, preferred_element_type=F32)


def turned(block):
    stacked = jnp.concatenate(
        [block[:, q * LANES : (q + 1) * LANES] for q in range(PER)], axis=0
    )
    return jnp.swapaxes(stacked, 0, 1)


def local_kernel(
    features, window, up, radial_w, out_w, read_w, senders, live, harm, radial, species, cot,
    energy_ref, d_upd_ref, d_own_ref, d_win_ref, grads_ref,
    table, low, high, low16, high16, half, y_t, r_t, w_ref, hot_rows, onehot, lhs, mixed, d_inv, inv, acc, gath, back, d_mix, rad_acc,
):
    up_v = up[...]
    own = mm(features[...], up_v, NN).astype(BF16)
    win = mm(window[...], up_v, NN).astype(BF16)
    table[0:ATOMS, 0:C] = own
    table[ATOMS:HALF, 0:C] = win[0 : HALF - ATOMS, :]
    table[:, C : 2 * C] = win[HALF - ATOMS :, :]

    send = turned(senders[...].astype(F32))
    second = (send >= HALF).astype(F32)
    within = send - second * HALF
    half[...] = second
    tens = jnp.floor(within * (1.0 / 16))
    high16[...] = tens
    low16[...] = within - tens * 16
    hundreds = jnp.floor(send * (1.0 / LANES))
    high[...] = hundreds
    low[...] = send - hundreds * LANES
    alive = live[...].astype(F32)
    for m in range(PARTS):
        y_t[m] = turned(harm[m].astype(F32) * alive)
    for n in range(BASIS):
        r_t[n] = turned(radial[n].astype(F32))

    for n in range(BASIS):
        for l in range(3):
            w_ref[n * 3 + l] = jnp.broadcast_to(
                radial_w[n : n + 1, l * C : (l + 1) * C].astype(F32), (8, C)
            )

    for q in range(PER):
        kind = jnp.swapaxes(jnp.broadcast_to(species[q : q + 1, :], (LANES, LANES)), 0, 1)
        weight = jnp.swapaxes(jnp.broadcast_to(cot[q : q + 1, :], (LANES, LANES)), 0, 1)
        readout = jnp.zeros((LANES, C), F32)
        for t in range(4):
            readout = jnp.where(kind == t, read_w[t : t + 1, :], readout)
        d_upd = weight * readout
        d_upd_ref[q * LANES : (q + 1) * LANES, :] = d_upd
        d_part = mm(d_upd.astype(BF16), out_w[...], NT)
        for l in range(3):
            d_inv[l, q * LANES : (q + 1) * LANES, :] = d_part[:, l * C : (l + 1) * C]

    acc[...] = jnp.zeros_like(acc)
    rad_acc[...] = jnp.zeros_like(rad_acc)

    sub16 = lax.broadcasted_iota(jnp.int32, (16, EDGES), 0)
    lane16 = lax.broadcasted_iota(jnp.int32, (16, EDGES), 1)
    owner = (sub16 & 7) == (lane16 >> 5)
    sub16f = sub16.astype(F32).astype(BF16)
    norm = 1.0 / math.sqrt(SLOTS)

    lane_b = lax.broadcasted_iota(jnp.int32, (EDGES, LANES), 1).astype(F32).astype(BF16)

    def step(i, carry):
        for g in range(BATCH):
            a = i * BATCH + g
            rows = slice(g * EDGES, (g + 1) * EDGES)
            lo = jnp.swapaxes(jnp.broadcast_to(low[pl.ds(a, 1), :], (LANES, EDGES)).astype(BF16), 0, 1)
            hi = jnp.swapaxes(jnp.broadcast_to(high[pl.ds(a, 1), :], (LANES, EDGES)).astype(BF16), 0, 1)
            upper = hi >= HALF // LANES
            z = jnp.where(lo == lane_b, jnp.where(upper, hi - HALF // LANES, hi), jnp.full_like(hi, -1))
            for block in range(HALF // LANES):
                hot_rows[rows, block * LANES : (block + 1) * LANES] = jnp.where(
                    z == block, jnp.ones_like(z), jnp.zeros_like(z)
                )
            both = mm(hot_rows[rows, :], table[...], NN)
            gath[rows, :] = jnp.where(upper, both[:, C:].astype(BF16), both[:, :C].astype(BF16))
        for g in range(BATCH):
            a = i * BATCH + g
            cols = slice(g * EDGES, (g + 1) * EDGES)
            lo = jnp.broadcast_to(low16[pl.ds(a, 1), :], (16, EDGES)).astype(BF16)
            hi = jnp.broadcast_to(high16[pl.ds(a, 1), :], (16, EDGES)).astype(BF16)
            z = jnp.where(lo == sub16f, hi, jnp.full_like(hi, -1))
            for block in range(HALF // 16):
                onehot[block * 16 : block * 16 + 16, cols] = jnp.where(
                    z == block, jnp.ones_like(z), jnp.zeros_like(z)
                )
        for g in range(BATCH):
            a = i * BATCH + g
            r16 = []
            for j in range(BASIS // 2):
                r16.append(
                    jnp.concatenate(
                        [
                            jnp.broadcast_to(r_t[2 * j + k, pl.ds(a, 1), :], (8, EDGES))
                            for k in range(2)
                        ],
                        axis=0,
                    ).astype(BF16)
                )
            for m in range(PARTS):
                y16 = jnp.where(
                    owner, jnp.broadcast_to(y_t[m, pl.ds(a, 1), :], (16, EDGES)), 0.0
                ).astype(BF16)
                for j in range(BASIS // 2):
                    row = m * 64 + j * 16
                    lhs[g, row : row + 16, :] = y16 * r16[j]
        for g in range(BATCH):
            mixed[g] = mm(lhs[g], gath[g * EDGES : (g + 1) * EDGES, :], NN)
        for g in range(BATCH):
            a = i * BATCH + g
            amps = []
            for m in range(PARTS):
                total = None
                for n in range(BASIS):
                    term = mixed[g, m * 64 + n * 8 : m * 64 + n * 8 + 8, :] * w_ref[n * 3 + DEGREE[m]]
                    total = term if total is None else total + term
                amps.append(total * norm)
            inv1 = amps[1] * amps[1] + amps[2] * amps[2] + amps[3] * amps[3]
            inv2 = sum(amps[m] * amps[m] for m in range(5, 9)) + amps[4] * amps[4]
            for l, value in enumerate((amps[0], inv1, inv2)):
                inv[l, pl.ds(a, 8, stride=LANES), :] = value
            d_l = [d_inv[l, pl.ds(a, 8, stride=LANES), :] * norm for l in range(3)]
            d_amps = [d_l[0]]
            for m in range(1, PARTS):
                d_amps.append(2.0 * amps[m] * d_l[DEGREE[m]])
            for n in range(BASIS):
                for l in range(3):
                    total = None
                    for m in range(PARTS):
                        if DEGREE[m] != l:
                            continue
                        term = mixed[g, m * 64 + n * 8 : m * 64 + n * 8 + 8, :] * d_amps[m]
                        total = term if total is None else total + term
                    rad_acc[n * 3 + l] += total
            for m in range(PARTS):
                for j in range(BASIS // 2):
                    row = m * 64 + j * 16
                    d_mix[g, row : row + 16, :] = jnp.concatenate(
                        [d_amps[m] * w_ref[(2 * j + k) * 3 + DEGREE[m]] for k in range(2)], axis=0
                    ).astype(BF16)
        for g in range(BATCH):
            a = i * BATCH + g
            cols = slice(g * EDGES, (g + 1) * EDGES)
            second = jnp.broadcast_to(half[pl.ds(a, 1), :], (C, EDGES)) > 0.5
            d_t = mm(d_mix[g], lhs[g], TN)
            back[0:C, cols] = jnp.where(second, 0.0, d_t).astype(BF16)
            back[C : 2 * C, cols] = jnp.where(second, d_t, 0.0).astype(BF16)
        for first in range(0, HALF, CHUNK):
            rows = slice(first, first + CHUNK)
            acc[rows, :] += mm(onehot[rows, :], back[...], NT)
        return carry

    lax.fori_loop(0, LANES // BATCH, step, 0)

    d_out = jnp.zeros((3 * C, C), F32)
    read_rows = [jnp.zeros((1, C), F32) for _ in range(4)]
    for q in range(PER):
        rows = slice(q * LANES, (q + 1) * LANES)
        invariants = jnp.concatenate([inv[l, rows, :] for l in range(3)], axis=1).astype(BF16)
        updated = mm(invariants, out_w[...], NN) + features[rows, :].astype(F32)
        kind = jnp.swapaxes(jnp.broadcast_to(species[q : q + 1, :], (LANES, LANES)), 0, 1)
        weight = jnp.swapaxes(jnp.broadcast_to(cot[q : q + 1, :], (LANES, LANES)), 0, 1)
        readout = jnp.zeros((LANES, C), F32)
        for t in range(4):
            readout = jnp.where(kind == t, read_w[t : t + 1, :], readout)
            read_rows[t] = read_rows[t] + jnp.sum(
                jnp.where(kind == t, weight * updated, 0.0), axis=0, keepdims=True
            )
        energy_ref[q : q + 1, :] = jnp.sum(
            jnp.swapaxes(updated * readout, 0, 1), axis=0, keepdims=True
        )
        d_rounded = d_upd_ref[rows, :].astype(BF16)
        d_out = d_out + mm(invariants, d_rounded, TN)
    d_own = acc[0:ATOMS, 0:C]
    d_own_ref[...] = d_own
    d_win = jnp.concatenate([acc[ATOMS:HALF, 0:C], acc[:, C : 2 * C]], axis=0).astype(BF16)
    d_win_ref[...] = d_win
    up_sum = mm(features[...], d_own.astype(BF16), TN) + mm(window[...], d_win, TN)
    large = jnp.concatenate([up_sum, d_out], axis=0)
    blank = jnp.zeros((8, C), F32)
    for piece in range(16):
        if piece < 3:
            small = jnp.concatenate(
                [jnp.sum(rad_acc[n * 3 + piece], axis=0, keepdims=True) for n in range(BASIS)], axis=0
            )
        elif piece == 3:
            small = jnp.concatenate(read_rows + [jnp.zeros((4, C), F32)], axis=0)
        else:
            small = blank
        grads_ref[piece] = jnp.concatenate(
            [large[piece * 32 : piece * 32 + 32], small, blank], axis=0
        ).astype(BF16)


def local_terms(features, window, up, radial_w, out_w, read_w, senders, live, harm, radial, species, cot):
    vm = pl.BlockSpec(memory_space=pltpu.VMEM)
    return pl.pallas_call(
        local_kernel,
        out_shape=(
            jax.ShapeDtypeStruct((PER, LANES), F32),
            jax.ShapeDtypeStruct((ATOMS, C), F32),
            jax.ShapeDtypeStruct((ATOMS, C), F32),
            jax.ShapeDtypeStruct((WINDOW, C), BF16),
            jax.ShapeDtypeStruct((16, 48, C), BF16),
        ),
        in_specs=[vm] * 12,
        out_specs=(vm,) * 5,
        scratch_shapes=[
            pltpu.VMEM((HALF, 2 * C), BF16),
            pltpu.VMEM((LANES, EDGES), F32),
            pltpu.VMEM((LANES, EDGES), F32),
            pltpu.VMEM((LANES, EDGES), F32),
            pltpu.VMEM((LANES, EDGES), F32),
            pltpu.VMEM((LANES, EDGES), F32),
            pltpu.VMEM((PARTS, LANES, EDGES), F32),
            pltpu.VMEM((BASIS, LANES, EDGES), F32),
            pltpu.VMEM((3 * BASIS, 8, C), F32),
            pltpu.VMEM((BATCH * EDGES, HALF), BF16),
            pltpu.VMEM((HALF, BATCH * EDGES), BF16),
            pltpu.VMEM((BATCH, PARTS * BASIS * 8, EDGES), BF16),
            pltpu.VMEM((BATCH, PARTS * BASIS * 8, C), F32),
            pltpu.VMEM((3, ATOMS, C), F32),
            pltpu.VMEM((3, ATOMS, C), F32),
            pltpu.VMEM((HALF, 2 * C), F32),
            pltpu.VMEM((BATCH * EDGES, C), BF16),
            pltpu.VMEM((2 * C, BATCH * EDGES), BF16),
            pltpu.VMEM((BATCH, PARTS * BASIS * 8, C), BF16),
            pltpu.VMEM((3 * BASIS, 8, C), F32),
        ],
        compiler_params=pltpu.CompilerParams(vmem_limit_bytes=50 * 1024 * 1024),
    )(features, window, up, radial_w, out_w, read_w, senders, live, harm, radial, species, cot)


AXES = ("gx", "gy", "gz")
MESH = pl.DeviceIdType.MESH
GHOST = 32
PIECES = 16
PIECE_ROWS = 48


def place():
    return {axis: lax.axis_index(axis) for axis in AXES}


def shifted(axis, by):
    me = place()
    me[axis] = lax.rem(me[axis] + by + lax.axis_size(axis), lax.axis_size(axis))
    return tuple(me[name] for name in AXES)


def remote(source, target, send, arrive, device):
    return pltpu.make_async_remote_copy(
        src_ref=source,
        dst_ref=target,
        send_sem=send,
        recv_sem=arrive,
        device_id=device,
        device_id_type=MESH,
    )


def column(row):
    return jnp.swapaxes(jnp.broadcast_to(row, (LANES, LANES)), 0, 1)


def spread_kernel(features, ghost, window, send, arrive):
    barrier = pltpu.get_barrier_semaphore()
    for axis in AXES:
        for by in (1, -1):
            pl.semaphore_signal(barrier, inc=1, device_id=shifted(axis, by), device_id_type=MESH)
    lane = lax.broadcasted_iota(jnp.int32, (LANES, LANES), 1)
    for h in range(2):
        rows = column(ghost[h : h + 1, :])
        hot = jnp.concatenate(
            [
                jnp.where(rows == lane + block * LANES, 1.0, 0.0).astype(BF16)
                for block in range(ATOMS // LANES)
            ],
            axis=1,
        )
        picked = mm(hot, features[...], NN).astype(BF16)
        for j in range(2):
            for k in range(2):
                first = (j * 2 + k) * GHOST
                window[1 + h, 1 + j, 1 + k] = picked[first : first + GHOST, :]
    pl.semaphore_wait(barrier, 6)
    inner = pl.ds(1, 2)
    plans = (
        ("gy", lambda at: window.at[inner, at, inner]),
        ("gx", lambda at: window.at[at, :, inner]),
        ("gz", lambda at: window.at[:, :, at]),
    )
    for number, (axis, view) in enumerate(plans):
        up = remote(
            view(2), view(0), send.at[2 * number], arrive.at[2 * number], shifted(axis, 1)
        )
        down = remote(
            view(1), view(3), send.at[2 * number + 1], arrive.at[2 * number + 1], shifted(axis, -1)
        )
        up.start()
        down.start()
        up.wait()
        down.wait()


def spread(features, ghost):
    vm = pl.BlockSpec(memory_space=pltpu.VMEM)
    return pl.pallas_call(
        spread_kernel,
        out_shape=jax.ShapeDtypeStruct((4, 4, 4, GHOST, C), BF16),
        in_specs=[vm] * 2,
        out_specs=vm,
        scratch_shapes=[pltpu.SemaphoreType.DMA((6,)), pltpu.SemaphoreType.DMA((6,))],
        compiler_params=pltpu.CompilerParams(
            collective_id=0, has_side_effects=True, vmem_limit_bytes=8 * 1024 * 1024
        ),
    )(features, ghost)


def plane_device(by):
    return shifted("gz", by)


def stack_device(by):
    me = place()
    wide = lax.axis_size("gy")
    count = lax.axis_size("gx") * wide
    other = lax.rem(me["gx"] * wide + me["gy"] + by, count)
    return (lax.div(other, wide), lax.rem(other, wide), me["gz"]), other


def finish_kernel(
    scale, d_win, grads, d_own, d_upd, ghost, up,
    feature_grad, up_grad, rad_grad, out_grad, read_grad,
    from_z, from_x, from_y, wide, narrow, first, second, third, hot,
    near_send, near_arrive, send1, arrive1, send2, arrive2, send3, arrive3,
):
    me = place()
    k = me["gz"]
    s = me["gx"] * lax.axis_size("gy") + me["gy"]

    barrier = pltpu.get_barrier_semaphore()

    def greet(by, carry):
        pl.semaphore_signal(barrier, inc=1, device_id=plane_device(by), device_id_type=MESH)
        pl.semaphore_signal(barrier, inc=1, device_id=stack_device(by)[0], device_id_type=MESH)
        return carry

    lax.fori_loop(1, PIECES, greet, 0)
    pl.semaphore_wait(barrier, 2 * (PIECES - 1))

    def near(number, low_view, high_view, landing, axis):
        down = remote(
            low_view, landing.at[0], near_send.at[2 * number], near_arrive.at[2 * number],
            shifted(axis, -1),
        )
        above = remote(
            high_view, landing.at[1], near_send.at[2 * number + 1], near_arrive.at[2 * number + 1],
            shifted(axis, 1),
        )
        down.start()
        above.start()
        return down, above

    copies_z = near(0, d_win.at[:, :, 0], d_win.at[:, :, 3], from_z, "gz")

    def copy1(by):
        target = lax.rem(k + by, PIECES)
        return remote(
            grads.at[target], first.at[k], send1.at[target], arrive1.at[k], plane_device(by)
        )

    def copy2(by):
        device, other = stack_device(by)
        return remote(second.at[s], second.at[s], send2.at[other], arrive2.at[s], device)

    def copy3(by):
        target = lax.rem(k + by, PIECES)
        return remote(third.at[k], third.at[k], send3.at[target], arrive3.at[k], plane_device(by))

    def started(copy):
        def body(by, carry):
            copy(by).start()
            return carry

        lax.fori_loop(1, PIECES, body, 0)

    def settled(copy, slots, sems, mine):
        def body(by, carry):
            copy(by).wait_send()
            source = lax.rem(mine + by, PIECES)
            remote(
                slots.at[source], slots.at[source], sems.at[source], sems.at[source],
                plane_device(1),
            ).wait_recv()
            return carry

        lax.fori_loop(1, PIECES, body, 0)

    started(copy1)
    first[k] = grads[k]
    atom = lax.broadcasted_iota(jnp.int32, (ATOMS, LANES), 0)
    for h in range(2):
        hot[h] = jnp.where(atom == ghost[h : h + 1, :], 1.0, 0.0).astype(BF16)
    feature_grad[...] = mm(d_own[...].astype(BF16), up[...], NT) + d_upd[...]

    for copy in copies_z:
        copy.wait()
    wide[:, :, 0] = (d_win[:, :, 1].astype(F32) + from_z[1].astype(F32)).astype(BF16)
    wide[:, :, 1] = (d_win[:, :, 2].astype(F32) + from_z[0].astype(F32)).astype(BF16)
    copies_x = near(1, wide.at[0], wide.at[3], from_x, "gx")

    settled(copy1, first, arrive1, k)
    second[s] = sum_of(first)
    started(copy2)

    for copy in copies_x:
        copy.wait()
    narrow[0] = (wide[1].astype(F32) + from_x[1].astype(F32)).astype(BF16)
    narrow[1] = (wide[2].astype(F32) + from_x[0].astype(F32)).astype(BF16)
    copies_y = near(2, narrow.at[:, 0], narrow.at[:, 3], from_y, "gy")

    settled(copy2, second, arrive2, s)
    third[k] = sum_of(second)
    started(copy3)

    for copy in copies_y:
        copy.wait()
    for h in range(2):
        sides = (
            narrow[h, 1].astype(F32) + from_y[1, h].astype(F32),
            narrow[h, 2].astype(F32) + from_y[0, h].astype(F32),
        )
        folded = jnp.concatenate([side.reshape(2 * GHOST, C) for side in sides], axis=0).astype(BF16)
        returned = mm(folded, up[...], NT).astype(BF16)
        feature_grad[...] += mm(hot[h], returned, NN)

    settled(copy3, third, arrive3, k)
    for piece in range(4):
        up_grad[piece * 32 : piece * 32 + 32, :] = third[piece, 0:32].astype(F32) * scale
    for piece in range(12):
        out_grad[piece * 32 : piece * 32 + 32, :] = third[4 + piece, 0:32].astype(F32) * scale
    for l in range(3):
        rad_grad[:, l * C : (l + 1) * C] = third[l, 32:48].astype(F32)[0:8] * scale
    read_grad[...] = third[3, 32:48].astype(F32)[0:4] * scale


def sum_of(slots):
    total = slots[0].astype(F32)
    for piece in range(1, PIECES):
        total = total + slots[piece].astype(F32)
    return total.astype(BF16)


def finish(scale, d_win, grads, d_own, d_upd, ghost, up):
    vm = pl.BlockSpec(memory_space=pltpu.VMEM)
    sems = pltpu.SemaphoreType.DMA((PIECES,))
    return pl.pallas_call(
        functools.partial(finish_kernel, scale),
        out_shape=(
            jax.ShapeDtypeStruct((ATOMS, C), F32),
            jax.ShapeDtypeStruct((C, C), F32),
            jax.ShapeDtypeStruct((BASIS, 3 * C), F32),
            jax.ShapeDtypeStruct((3 * C, C), F32),
            jax.ShapeDtypeStruct((4, C), F32),
        ),
        in_specs=[vm] * 6,
        out_specs=(vm,) * 5,
        scratch_shapes=[
            pltpu.VMEM((2, 4, 4, GHOST, C), BF16),
            pltpu.VMEM((2, 4, 2, GHOST, C), BF16),
            pltpu.VMEM((2, 2, 2, GHOST, C), BF16),
            pltpu.VMEM((4, 4, 2, GHOST, C), BF16),
            pltpu.VMEM((2, 4, 2, GHOST, C), BF16),
            pltpu.VMEM((PIECES, PIECE_ROWS, C), BF16),
            pltpu.VMEM((PIECES, PIECE_ROWS, C), BF16),
            pltpu.VMEM((PIECES, PIECE_ROWS, C), BF16),
            pltpu.VMEM((2, ATOMS, LANES), BF16),
            pltpu.SemaphoreType.DMA((6,)),
            pltpu.SemaphoreType.DMA((6,)),
            sems, sems, sems, sems, sems, sems,
        ],
        compiler_params=pltpu.CompilerParams(
            collective_id=1, has_side_effects=True, vmem_limit_bytes=16 * 1024 * 1024
        ),
    )(d_win, grads, d_own, d_upd, ghost, up)


def per_device(
    features, up_weight, radial_weight, out_weight, read_weight,
    ghost_rows, senders, live, harmonics, radial, species, cotangent,
):
    ghost = ghost_rows.reshape(2, LANES)
    window = spread(features, ghost)
    energy, d_upd, d_own, d_win, grads = local_terms(
        features, window.reshape(WINDOW, C), up_weight, radial_weight, out_weight, read_weight,
        senders, live, harmonics, radial,
        species.reshape(PER, LANES), cotangent.reshape(PER, LANES),
    )
    scale = 1.0 / math.sqrt(ATOMS * lax.axis_size("gx") * lax.axis_size("gy") * lax.axis_size("gz"))
    feature_grad, up_grad, rad_grad, out_grad, read_grad = finish(
        scale, d_win.reshape(4, 4, 4, GHOST, C), grads, d_own, d_upd, ghost, up_weight
    )
    return energy.reshape(ATOMS), feature_grad, up_grad, rad_grad, out_grad, read_grad


def solution(mesh):
    whole = P(AXES)
    in_specs = (
        P(AXES, None), P(), P(), P(), P(),
        P("gx", "gy", "gz", None), P(None, AXES), P(None, AXES), P(None, None, AXES),
        P(None, None, AXES), whole, whole,
    )
    out_specs = (whole, P(AXES, None), P(), P(), P(), P())
    return jax.shard_map(
        per_device, mesh=mesh, in_specs=in_specs, out_specs=out_specs, check_vma=False
    )
```

```python
import functools
import math

import jax
import jax.numpy as jnp
import numpy as np
from jax import lax
from jax.experimental import pallas as pl
from jax.experimental.pallas import tpu as pltpu
from jax.sharding import PartitionSpec as P

C = 128
LANES = 128
SLOTS = 32
ATOMS = 1024
BASIS = 8
PARTS = 9
WINDOW = 2048
INNER = tuple(p * 16 + q * 4 + r for p in (1, 2) for q in (1, 2) for r in (1, 2))
TABLE = ATOMS + WINDOW - 32 * len(INNER)
HALF = TABLE // 2
OUTER = ((0, 21), (23, 25), (27, 37), (39, 41), (43, 64))
PER = ATOMS // LANES
EDGES = PER * SLOTS
BATCH = 16
DEGREE = (0, 1, 1, 1, 2, 2, 2, 2, 2)
F32 = jnp.float32
BF16 = jnp.bfloat16

CHUNK = 352
NT = (((1,), (1,)), ((), ()))
TN = (((0,), (0,)), ((), ()))
NN = (((1,), (0,)), ((), ()))


def mm(a, b, dims):
    return lax.dot_general(a, b, dims, preferred_element_type=F32)


def turned(block):
    stacked = jnp.concatenate(
        [block[:, q * LANES : (q + 1) * LANES] for q in range(PER)], axis=0
    )
    return jnp.swapaxes(stacked, 0, 1)


def local_kernel(
    features, window, up, radial_w, out_w, read_w, senders, live, harm, radial, species, cot,
    energy_ref, d_upd_ref, d_own_ref, d_win_ref, grads_ref,
    table, low, high, low16, high16, half, y_t, r_t, w_ref, onehot, lhs, mixed, d_inv, inv, acc, gath, back, d_mix, rad_acc,
):
    up_v = up[...]
    own = mm(features[...], up_v, NN).astype(BF16)
    win = mm(window[...], up_v, NN).astype(BF16)
    table[0:ATOMS, 0:C] = own
    outer = jnp.concatenate([win[first * 32 : last * 32] for first, last in OUTER], axis=0)
    table[ATOMS:HALF, 0:C] = outer[0 : HALF - ATOMS, :]
    table[:, C : 2 * C] = outer[HALF - ATOMS :, :]

    send = turned(senders[...].astype(F32))
    named_row = send
    for cell in INNER:
        send = send - jnp.where(named_row >= ATOMS + 32 * (cell + 1), 32.0, 0.0)
    second = (send >= HALF).astype(F32)
    within = send - second * HALF
    half[...] = second
    tens = jnp.floor(within * (1.0 / 16))
    high16[...] = tens
    low16[...] = within - tens * 16
    hundreds = jnp.floor(send * (1.0 / LANES))
    high[...] = hundreds
    low[...] = send - hundreds * LANES
    alive = live[...].astype(F32)
    for m in range(PARTS):
        y_t[m] = turned(harm[m].astype(F32) * alive)
    for n in range(BASIS):
        r_t[n] = turned(radial[n].astype(F32))

    for n in range(BASIS):
        for l in range(3):
            w_ref[n * 3 + l] = jnp.broadcast_to(
                radial_w[n : n + 1, l * C : (l + 1) * C].astype(F32), (8, C)
            )

    for q in range(PER):
        kind = jnp.swapaxes(jnp.broadcast_to(species[q : q + 1, :], (LANES, LANES)), 0, 1)
        weight = jnp.swapaxes(jnp.broadcast_to(cot[q : q + 1, :], (LANES, LANES)), 0, 1)
        readout = jnp.zeros((LANES, C), F32)
        for t in range(4):
            readout = jnp.where(kind == t, read_w[t : t + 1, :], readout)
        d_upd = weight * readout
        d_upd_ref[q * LANES : (q + 1) * LANES, :] = d_upd
        d_part = mm(d_upd.astype(BF16), out_w[...], NT)
        for l in range(3):
            d_inv[l, q * LANES : (q + 1) * LANES, :] = d_part[:, l * C : (l + 1) * C]

    acc[...] = jnp.zeros_like(acc)
    rad_acc[...] = jnp.zeros_like(rad_acc)

    sub16 = lax.broadcasted_iota(jnp.int32, (16, EDGES), 0)
    lane16 = lax.broadcasted_iota(jnp.int32, (16, EDGES), 1)
    owner = (sub16 & 7) == (lane16 >> 5)
    sub16f = sub16.astype(F32).astype(BF16)
    norm = 1.0 / math.sqrt(SLOTS)

    lane_b = lax.broadcasted_iota(jnp.int32, (EDGES, LANES), 1).astype(F32).astype(BF16)

    def step(i, carry):
        for g in range(BATCH):
            a = i * BATCH + g
            rows = slice(g * EDGES, (g + 1) * EDGES)
            lo = jnp.swapaxes(jnp.broadcast_to(low[pl.ds(a, 1), :], (LANES, EDGES)).astype(BF16), 0, 1)
            hi = jnp.swapaxes(jnp.broadcast_to(high[pl.ds(a, 1), :], (LANES, EDGES)).astype(BF16), 0, 1)
            upper = hi >= HALF // LANES
            z = jnp.where(lo == lane_b, jnp.where(upper, hi - HALF // LANES, hi), jnp.full_like(hi, -1))
            named = jnp.concatenate(
                [
                    jnp.where(z == block, jnp.ones_like(z), jnp.zeros_like(z))
                    for block in range(HALF // LANES)
                ],
                axis=1,
            )
            both = mm(named, table[...], NN)
            gath[rows, :] = jnp.where(upper, both[:, C:].astype(BF16), both[:, :C].astype(BF16))
        for g in range(BATCH):
            a = i * BATCH + g
            cols = slice(g * EDGES, (g + 1) * EDGES)
            lo = jnp.broadcast_to(low16[pl.ds(a, 1), :], (16, EDGES)).astype(BF16)
            hi = jnp.broadcast_to(high16[pl.ds(a, 1), :], (16, EDGES)).astype(BF16)
            z = jnp.where(lo == sub16f, hi, jnp.full_like(hi, -1))
            for block in range(HALF // 16):
                onehot[block * 16 : block * 16 + 16, cols] = jnp.where(
                    z == block, jnp.ones_like(z), jnp.zeros_like(z)
                )
        for g in range(BATCH):
            a = i * BATCH + g
            r16 = []
            for j in range(BASIS // 2):
                r16.append(
                    jnp.concatenate(
                        [
                            jnp.broadcast_to(r_t[2 * j + k, pl.ds(a, 1), :], (8, EDGES))
                            for k in range(2)
                        ],
                        axis=0,
                    ).astype(BF16)
                )
            for m in range(PARTS):
                y16 = jnp.where(
                    owner, jnp.broadcast_to(y_t[m, pl.ds(a, 1), :], (16, EDGES)), 0.0
                ).astype(BF16)
                for j in range(BASIS // 2):
                    row = m * 64 + j * 16
                    lhs[g, row : row + 16, :] = y16 * r16[j]
        for g in range(BATCH):
            mixed[g] = mm(lhs[g], gath[g * EDGES : (g + 1) * EDGES, :], NN)
        for g in range(BATCH):
            a = i * BATCH + g
            amps = []
            for m in range(PARTS):
                total = None
                for n in range(BASIS):
                    term = mixed[g, m * 64 + n * 8 : m * 64 + n * 8 + 8, :] * w_ref[n * 3 + DEGREE[m]]
                    total = term if total is None else total + term
                amps.append(total * norm)
            inv1 = amps[1] * amps[1] + amps[2] * amps[2] + amps[3] * amps[3]
            inv2 = sum(amps[m] * amps[m] for m in range(5, 9)) + amps[4] * amps[4]
            for l, value in enumerate((amps[0], inv1, inv2)):
                inv[l, pl.ds(a, 8, stride=LANES), :] = value
            d_l = [d_inv[l, pl.ds(a, 8, stride=LANES), :] * norm for l in range(3)]
            d_amps = [d_l[0]]
            for m in range(1, PARTS):
                d_amps.append(2.0 * amps[m] * d_l[DEGREE[m]])
            for n in range(BASIS):
                for l in range(3):
                    total = None
                    for m in range(PARTS):
                        if DEGREE[m] != l:
                            continue
                        term = mixed[g, m * 64 + n * 8 : m * 64 + n * 8 + 8, :] * d_amps[m]
                        total = term if total is None else total + term
                    rad_acc[n * 3 + l] += total
            for m in range(PARTS):
                for j in range(BASIS // 2):
                    row = m * 64 + j * 16
                    d_mix[g, row : row + 16, :] = jnp.concatenate(
                        [d_amps[m] * w_ref[(2 * j + k) * 3 + DEGREE[m]] for k in range(2)], axis=0
                    ).astype(BF16)
        for g in range(BATCH):
            a = i * BATCH + g
            cols = slice(g * EDGES, (g + 1) * EDGES)
            second = jnp.broadcast_to(half[pl.ds(a, 1), :], (C, EDGES)) > 0.5
            d_t = mm(d_mix[g], lhs[g], TN)
            back[0:C, cols] = jnp.where(second, 0.0, d_t).astype(BF16)
            back[C : 2 * C, cols] = jnp.where(second, d_t, 0.0).astype(BF16)
        for first in range(0, HALF, CHUNK):
            rows = slice(first, first + CHUNK)
            acc[rows, :] += mm(onehot[rows, :], back[...], NT)
        return carry

    lax.fori_loop(0, LANES // BATCH, step, 0)

    d_out = jnp.zeros((3 * C, C), F32)
    read_rows = [jnp.zeros((1, C), F32) for _ in range(4)]
    for q in range(PER):
        rows = slice(q * LANES, (q + 1) * LANES)
        invariants = jnp.concatenate([inv[l, rows, :] for l in range(3)], axis=1).astype(BF16)
        updated = mm(invariants, out_w[...], NN) + features[rows, :].astype(F32)
        kind = jnp.swapaxes(jnp.broadcast_to(species[q : q + 1, :], (LANES, LANES)), 0, 1)
        weight = jnp.swapaxes(jnp.broadcast_to(cot[q : q + 1, :], (LANES, LANES)), 0, 1)
        readout = jnp.zeros((LANES, C), F32)
        for t in range(4):
            readout = jnp.where(kind == t, read_w[t : t + 1, :], readout)
            read_rows[t] = read_rows[t] + jnp.sum(
                jnp.where(kind == t, weight * updated, 0.0), axis=0, keepdims=True
            )
        energy_ref[q : q + 1, :] = jnp.sum(
            jnp.swapaxes(updated * readout, 0, 1), axis=0, keepdims=True
        )
        d_rounded = d_upd_ref[rows, :].astype(BF16)
        d_out = d_out + mm(invariants, d_rounded, TN)
    d_own = acc[0:ATOMS, 0:C]
    d_own_ref[...] = d_own
    d_outer = jnp.concatenate([acc[ATOMS:HALF, 0:C], acc[:, C : 2 * C]], axis=0).astype(BF16)
    d_win_ref[...] = jnp.zeros_like(d_win_ref)
    done = 0
    for first, last in OUTER:
        count = (last - first) * 32
        d_win_ref[first * 32 : last * 32, :] = d_outer[done : done + count]
        done += count
    d_win = d_win_ref[...]
    up_sum = mm(features[...], d_own.astype(BF16), TN) + mm(window[...], d_win, TN)
    large = jnp.concatenate([up_sum, d_out], axis=0)
    blank = jnp.zeros((8, C), F32)
    for piece in range(16):
        if piece < 3:
            small = jnp.concatenate(
                [jnp.sum(rad_acc[n * 3 + piece], axis=0, keepdims=True) for n in range(BASIS)], axis=0
            )
        elif piece == 3:
            small = jnp.concatenate(read_rows + [jnp.zeros((4, C), F32)], axis=0)
        else:
            small = blank
        grads_ref[piece] = jnp.concatenate(
            [large[piece * 32 : piece * 32 + 32], small, blank], axis=0
        ).astype(BF16)


def local_terms(features, window, up, radial_w, out_w, read_w, senders, live, harm, radial, species, cot):
    vm = pl.BlockSpec(memory_space=pltpu.VMEM)
    return pl.pallas_call(
        local_kernel,
        out_shape=(
            jax.ShapeDtypeStruct((PER, LANES), F32),
            jax.ShapeDtypeStruct((ATOMS, C), F32),
            jax.ShapeDtypeStruct((ATOMS, C), F32),
            jax.ShapeDtypeStruct((WINDOW, C), BF16),
            jax.ShapeDtypeStruct((16, 48, C), BF16),
        ),
        in_specs=[vm] * 12,
        out_specs=(vm,) * 5,
        scratch_shapes=[
            pltpu.VMEM((HALF, 2 * C), BF16),
            pltpu.VMEM((LANES, EDGES), F32),
            pltpu.VMEM((LANES, EDGES), F32),
            pltpu.VMEM((LANES, EDGES), F32),
            pltpu.VMEM((LANES, EDGES), F32),
            pltpu.VMEM((LANES, EDGES), F32),
            pltpu.VMEM((PARTS, LANES, EDGES), F32),
            pltpu.VMEM((BASIS, LANES, EDGES), F32),
            pltpu.VMEM((3 * BASIS, 8, C), F32),
            pltpu.VMEM((HALF, BATCH * EDGES), BF16),
            pltpu.VMEM((BATCH, PARTS * BASIS * 8, EDGES), BF16),
            pltpu.VMEM((BATCH, PARTS * BASIS * 8, C), F32),
            pltpu.VMEM((3, ATOMS, C), F32),
            pltpu.VMEM((3, ATOMS, C), F32),
            pltpu.VMEM((HALF, 2 * C), F32),
            pltpu.VMEM((BATCH * EDGES, C), BF16),
            pltpu.VMEM((2 * C, BATCH * EDGES), BF16),
            pltpu.VMEM((BATCH, PARTS * BASIS * 8, C), BF16),
            pltpu.VMEM((3 * BASIS, 8, C), F32),
        ],
        compiler_params=pltpu.CompilerParams(vmem_limit_bytes=60 * 1024 * 1024),
    )(features, window, up, radial_w, out_w, read_w, senders, live, harm, radial, species, cot)


AXES = ("gx", "gy", "gz")
MESH = pl.DeviceIdType.MESH
GHOST = 32
PIECES = 16
PIECE_ROWS = 48


def place():
    return {axis: lax.axis_index(axis) for axis in AXES}


def shifted(axis, by):
    me = place()
    me[axis] = lax.rem(me[axis] + by + lax.axis_size(axis), lax.axis_size(axis))
    return tuple(me[name] for name in AXES)


def remote(source, target, send, arrive, device):
    return pltpu.make_async_remote_copy(
        src_ref=source,
        dst_ref=target,
        send_sem=send,
        recv_sem=arrive,
        device_id=device,
        device_id_type=MESH,
    )


def column(row):
    return jnp.swapaxes(jnp.broadcast_to(row, (LANES, LANES)), 0, 1)


def spread_kernel(features, ghost_rows, window, ghost, send, arrive):
    barrier = pltpu.get_barrier_semaphore()
    for axis in AXES:
        for by in (1, -1):
            pl.semaphore_signal(barrier, inc=1, device_id=shifted(axis, by), device_id_type=MESH)
    lane = lax.broadcasted_iota(jnp.int32, (LANES, LANES), 1)
    for h in range(2):
        row = jnp.concatenate(
            [ghost_rows[h, j, k : k + 1, :] for j in range(2) for k in range(2)], axis=1
        )
        ghost[h : h + 1, :] = row
        rows = column(row)
        hot = jnp.concatenate(
            [
                jnp.where(rows == lane + block * LANES, 1.0, 0.0).astype(BF16)
                for block in range(ATOMS // LANES)
            ],
            axis=1,
        )
        picked = mm(hot, features[...], NN).astype(BF16)
        for j in range(2):
            for k in range(2):
                first = (j * 2 + k) * GHOST
                window[1 + h, 1 + j, 1 + k] = picked[first : first + GHOST, :]
    pl.semaphore_wait(barrier, 6)
    inner = pl.ds(1, 2)
    plans = (
        ("gy", lambda at: window.at[inner, at, inner]),
        ("gx", lambda at: window.at[at, :, inner]),
        ("gz", lambda at: window.at[:, :, at]),
    )
    for number, (axis, view) in enumerate(plans):
        up = remote(
            view(2), view(0), send.at[2 * number], arrive.at[2 * number], shifted(axis, 1)
        )
        down = remote(
            view(1), view(3), send.at[2 * number + 1], arrive.at[2 * number + 1], shifted(axis, -1)
        )
        up.start()
        down.start()
        up.wait()
        down.wait()


def spread(features, ghost_rows):
    vm = pl.BlockSpec(memory_space=pltpu.VMEM)
    return pl.pallas_call(
        spread_kernel,
        out_shape=(
            jax.ShapeDtypeStruct((4, 4, 4, GHOST, C), BF16),
            jax.ShapeDtypeStruct((2, LANES), jnp.int32),
        ),
        in_specs=[vm] * 2,
        out_specs=(vm,) * 2,
        cost_estimate=pl.CostEstimate(
            flops=2 * 256 * ATOMS * C, bytes_accessed=60_000_000, transcendentals=0
        ),
        scratch_shapes=[pltpu.SemaphoreType.DMA((6,)), pltpu.SemaphoreType.DMA((6,))],
        compiler_params=pltpu.CompilerParams(
            collective_id=0, has_side_effects=True, vmem_limit_bytes=60 * 1024 * 1024
        ),
    )(features, ghost_rows)


def plane_device(by):
    return shifted("gz", by)


def stack_device(by):
    me = place()
    wide = lax.axis_size("gy")
    count = lax.axis_size("gx") * wide
    other = lax.rem(me["gx"] * wide + me["gy"] + by, count)
    return (lax.div(other, wide), lax.rem(other, wide), me["gz"]), other


def finish_kernel(
    scale, d_win, grads, d_own, d_upd, ghost, up,
    feature_grad, up_grad, rad_grad, out_grad, read_grad,
    from_z, from_x, from_y, wide, narrow, first, second, third, hot,
    near_send, near_arrive, send1, arrive1, send2, arrive2, send3, arrive3,
):
    me = place()
    k = me["gz"]
    s = me["gx"] * lax.axis_size("gy") + me["gy"]

    barrier = pltpu.get_barrier_semaphore()

    def greet(by, carry):
        pl.semaphore_signal(barrier, inc=1, device_id=plane_device(by), device_id_type=MESH)
        pl.semaphore_signal(barrier, inc=1, device_id=stack_device(by)[0], device_id_type=MESH)
        return carry

    lax.fori_loop(1, PIECES, greet, 0)
    pl.semaphore_wait(barrier, 2 * (PIECES - 1))

    def near(number, low_view, high_view, landing, axis):
        down = remote(
            low_view, landing.at[0], near_send.at[2 * number], near_arrive.at[2 * number],
            shifted(axis, -1),
        )
        above = remote(
            high_view, landing.at[1], near_send.at[2 * number + 1], near_arrive.at[2 * number + 1],
            shifted(axis, 1),
        )
        down.start()
        above.start()
        return down, above

    copies_z = near(0, d_win.at[:, :, 0], d_win.at[:, :, 3], from_z, "gz")

    def copy1(by):
        target = lax.rem(k + by, PIECES)
        return remote(
            grads.at[target], first.at[k], send1.at[target], arrive1.at[k], plane_device(by)
        )

    def copy2(by):
        device, other = stack_device(by)
        return remote(second.at[s], second.at[s], send2.at[other], arrive2.at[s], device)

    def copy3(by):
        target = lax.rem(k + by, PIECES)
        return remote(third.at[k], third.at[k], send3.at[target], arrive3.at[k], plane_device(by))

    def started(copy):
        def body(by, carry):
            copy(by).start()
            return carry

        lax.fori_loop(1, PIECES, body, 0)

    def settled(copy, slots, sems, mine):
        def body(by, carry):
            copy(by).wait_send()
            source = lax.rem(mine + by, PIECES)
            remote(
                slots.at[source], slots.at[source], sems.at[source], sems.at[source],
                plane_device(1),
            ).wait_recv()
            return carry

        lax.fori_loop(1, PIECES, body, 0)

    started(copy1)
    first[k] = grads[k]
    atom = lax.broadcasted_iota(jnp.int32, (ATOMS, LANES), 0)
    for h in range(2):
        hot[h] = jnp.where(atom == ghost[h : h + 1, :], 1.0, 0.0).astype(BF16)
    feature_grad[...] = mm(d_own[...].astype(BF16), up[...], NT) + d_upd[...]

    for copy in copies_z:
        copy.wait()
    wide[:, :, 0] = (d_win[:, :, 1].astype(F32) + from_z[1].astype(F32)).astype(BF16)
    wide[:, :, 1] = (d_win[:, :, 2].astype(F32) + from_z[0].astype(F32)).astype(BF16)
    copies_x = near(1, wide.at[0], wide.at[3], from_x, "gx")

    settled(copy1, first, arrive1, k)
    second[s] = sum_of(first)
    started(copy2)

    for copy in copies_x:
        copy.wait()
    narrow[0] = (wide[1].astype(F32) + from_x[1].astype(F32)).astype(BF16)
    narrow[1] = (wide[2].astype(F32) + from_x[0].astype(F32)).astype(BF16)
    copies_y = near(2, narrow.at[:, 0], narrow.at[:, 3], from_y, "gy")

    settled(copy2, second, arrive2, s)
    third[k] = sum_of(second)
    started(copy3)

    for copy in copies_y:
        copy.wait()
    for h in range(2):
        sides = (
            narrow[h, 1].astype(F32) + from_y[1, h].astype(F32),
            narrow[h, 2].astype(F32) + from_y[0, h].astype(F32),
        )
        folded = jnp.concatenate([side.reshape(2 * GHOST, C) for side in sides], axis=0).astype(BF16)
        returned = mm(folded, up[...], NT).astype(BF16)
        feature_grad[...] += mm(hot[h], returned, NN)

    settled(copy3, third, arrive3, k)
    for piece in range(4):
        up_grad[piece * 32 : piece * 32 + 32, :] = third[piece, 0:32].astype(F32) * scale
    for piece in range(12):
        out_grad[piece * 32 : piece * 32 + 32, :] = third[4 + piece, 0:32].astype(F32) * scale
    for l in range(3):
        rad_grad[:, l * C : (l + 1) * C] = third[l, 32:48].astype(F32)[0:8] * scale
    read_grad[...] = third[3, 32:48].astype(F32)[0:4] * scale


def sum_of(slots):
    total = slots[0].astype(F32)
    for piece in range(1, PIECES):
        total = total + slots[piece].astype(F32)
    return total.astype(BF16)


def finish(scale, d_win, grads, d_own, d_upd, ghost, up):
    vm = pl.BlockSpec(memory_space=pltpu.VMEM)
    sems = pltpu.SemaphoreType.DMA((PIECES,))
    return pl.pallas_call(
        functools.partial(finish_kernel, scale),
        out_shape=(
            jax.ShapeDtypeStruct((ATOMS, C), F32),
            jax.ShapeDtypeStruct((C, C), F32),
            jax.ShapeDtypeStruct((BASIS, 3 * C), F32),
            jax.ShapeDtypeStruct((3 * C, C), F32),
            jax.ShapeDtypeStruct((4, C), F32),
        ),
        in_specs=[vm] * 6,
        out_specs=(vm,) * 5,
        scratch_shapes=[
            pltpu.VMEM((2, 4, 4, GHOST, C), BF16),
            pltpu.VMEM((2, 4, 2, GHOST, C), BF16),
            pltpu.VMEM((2, 2, 2, GHOST, C), BF16),
            pltpu.VMEM((4, 4, 2, GHOST, C), BF16),
            pltpu.VMEM((2, 4, 2, GHOST, C), BF16),
            pltpu.VMEM((PIECES, PIECE_ROWS, C), BF16),
            pltpu.VMEM((PIECES, PIECE_ROWS, C), BF16),
            pltpu.VMEM((PIECES, PIECE_ROWS, C), BF16),
            pltpu.VMEM((2, ATOMS, LANES), BF16),
            pltpu.SemaphoreType.DMA((6,)),
            pltpu.SemaphoreType.DMA((6,)),
            sems, sems, sems, sems, sems, sems,
        ],
        compiler_params=pltpu.CompilerParams(
            collective_id=1, has_side_effects=True, vmem_limit_bytes=60 * 1024 * 1024
        ),
    )(d_win, grads, d_own, d_upd, ghost, up)


def per_device(
    features, up_weight, radial_weight, out_weight, read_weight,
    ghost_rows, senders, live, harmonics, radial, species, cotangent,
):
    window, ghost = spread(features, ghost_rows)
    energy, d_upd, d_own, d_win, grads = local_terms(
        features, window.reshape(WINDOW, C), up_weight, radial_weight, out_weight, read_weight,
        senders, live, harmonics, radial,
        species.reshape(PER, LANES), cotangent.reshape(PER, LANES),
    )
    scale = 1.0 / math.sqrt(ATOMS * lax.axis_size("gx") * lax.axis_size("gy") * lax.axis_size("gz"))
    feature_grad, up_grad, rad_grad, out_grad, read_grad = finish(
        scale, d_win.reshape(4, 4, 4, GHOST, C), grads, d_own, d_upd, ghost, up_weight
    )
    return energy.reshape(ATOMS), feature_grad, up_grad, rad_grad, out_grad, read_grad


def solution(mesh):
    whole = P(AXES)
    in_specs = (
        P(AXES, None), P(), P(), P(), P(),
        P("gx", "gy", "gz", None), P(None, AXES), P(None, AXES), P(None, None, AXES),
        P(None, None, AXES), whole, whole,
    )
    out_specs = (whole, P(AXES, None), P(), P(), P(), P())
    return jax.shard_map(
        per_device, mesh=mesh, in_specs=in_specs, out_specs=out_specs, check_vma=False
    )
```

```python
import functools
import math

import jax
import jax.numpy as jnp
import numpy as np
from jax import lax
from jax.experimental import pallas as pl
from jax.experimental.pallas import tpu as pltpu
from jax.sharding import PartitionSpec as P

C = 128
LANES = 128
SLOTS = 32
ATOMS = 1024
BASIS = 8
PARTS = 9
WINDOW = 2048
INNER = tuple(p * 16 + q * 4 + r for p in (1, 2) for q in (1, 2) for r in (1, 2))
TABLE = ATOMS + WINDOW - 32 * len(INNER)
HALF = TABLE // 2
OUTER = ((0, 21), (23, 25), (27, 37), (39, 41), (43, 64))
PER = ATOMS // LANES
EDGES = PER * SLOTS
BATCH = 16
DEGREE = (0, 1, 1, 1, 2, 2, 2, 2, 2)
F32 = jnp.float32
BF16 = jnp.bfloat16

CHUNK = 352
NT = (((1,), (1,)), ((), ()))
TN = (((0,), (0,)), ((), ()))
NN = (((1,), (0,)), ((), ()))


def mm(a, b, dims):
    return lax.dot_general(a, b, dims, preferred_element_type=F32)


def turned(block):
    stacked = jnp.concatenate(
        [block[:, q * LANES : (q + 1) * LANES] for q in range(PER)], axis=0
    )
    return jnp.swapaxes(stacked, 0, 1)


def local_kernel(
    features, window, up, radial_w, out_w, read_w, senders, live, harm, radial, species, cot,
    energy_ref, d_upd_ref, d_own_ref, d_win_ref, grads_ref,
    table, low, high, low16, high16, half, y_t, r_t, w_ref, onehot, lhs, mixed, d_inv, inv, acc, gath, back, d_mix, rad_acc,
):
    up_v = up[...]
    own = mm(features[...], up_v, NN).astype(BF16)
    win = mm(window[...], up_v, NN).astype(BF16)
    table[0:ATOMS, 0:C] = own
    outer = jnp.concatenate([win[first * 32 : last * 32] for first, last in OUTER], axis=0)
    table[ATOMS:HALF, 0:C] = outer[0 : HALF - ATOMS, :]
    table[:, C : 2 * C] = outer[HALF - ATOMS :, :]

    send = turned(senders[...].astype(F32))
    named_row = send
    for cell in INNER:
        send = send - jnp.where(named_row >= ATOMS + 32 * (cell + 1), 32.0, 0.0)
    second = (send >= HALF).astype(F32)
    within = send - second * HALF
    half[...] = second
    tens = jnp.floor(within * (1.0 / 16))
    high16[...] = tens
    low16[...] = within - tens * 16
    hundreds = jnp.floor(send * (1.0 / LANES))
    high[...] = hundreds
    low[...] = send - hundreds * LANES
    alive = live[...].astype(F32)
    for m in range(PARTS):
        y_t[m] = turned(harm[m].astype(F32) * alive)
    for n in range(BASIS):
        r_t[n] = turned(radial[n].astype(F32))

    for n in range(BASIS):
        for l in range(3):
            w_ref[n * 3 + l] = jnp.broadcast_to(
                radial_w[n : n + 1, l * C : (l + 1) * C].astype(F32), (8, C)
            )

    for q in range(PER):
        kind = jnp.swapaxes(jnp.broadcast_to(species[q : q + 1, :], (LANES, LANES)), 0, 1)
        weight = jnp.swapaxes(jnp.broadcast_to(cot[q : q + 1, :], (LANES, LANES)), 0, 1)
        readout = jnp.zeros((LANES, C), F32)
        for t in range(4):
            readout = jnp.where(kind == t, read_w[t : t + 1, :], readout)
        d_upd = weight * readout
        d_upd_ref[q * LANES : (q + 1) * LANES, :] = d_upd
        d_part = mm(d_upd.astype(BF16), out_w[...], NT)
        for l in range(3):
            d_inv[l, q * LANES : (q + 1) * LANES, :] = d_part[:, l * C : (l + 1) * C]

    acc[...] = jnp.zeros_like(acc)
    rad_acc[...] = jnp.zeros_like(rad_acc)

    sub16 = lax.broadcasted_iota(jnp.int32, (16, EDGES), 0)
    lane16 = lax.broadcasted_iota(jnp.int32, (16, EDGES), 1)
    owner = (sub16 & 7) == (lane16 >> 5)
    sub16f = sub16.astype(F32).astype(BF16)
    norm = 1.0 / math.sqrt(SLOTS)

    lane_b = lax.broadcasted_iota(jnp.int32, (EDGES, LANES), 1).astype(F32).astype(BF16)

    def step(i, carry):
        for g in range(BATCH):
            a = i * BATCH + g
            rows = slice(g * EDGES, (g + 1) * EDGES)
            lo = jnp.swapaxes(jnp.broadcast_to(low[pl.ds(a, 1), :], (LANES, EDGES)).astype(BF16), 0, 1)
            hi = jnp.swapaxes(jnp.broadcast_to(high[pl.ds(a, 1), :], (LANES, EDGES)).astype(BF16), 0, 1)
            upper = hi >= HALF // LANES
            z = jnp.where(lo == lane_b, jnp.where(upper, hi - HALF // LANES, hi), jnp.full_like(hi, -1))
            named = jnp.concatenate(
                [
                    jnp.where(z == block, jnp.ones_like(z), jnp.zeros_like(z))
                    for block in range(HALF // LANES)
                ],
                axis=1,
            )
            both = mm(named, table[...], NN)
            gath[rows, :] = jnp.where(upper, both[:, C:].astype(BF16), both[:, :C].astype(BF16))
        for g in range(BATCH):
            a = i * BATCH + g
            cols = slice(g * EDGES, (g + 1) * EDGES)
            lo = jnp.broadcast_to(low16[pl.ds(a, 1), :], (16, EDGES)).astype(BF16)
            hi = jnp.broadcast_to(high16[pl.ds(a, 1), :], (16, EDGES)).astype(BF16)
            z = jnp.where(lo == sub16f, hi, jnp.full_like(hi, -1))
            for block in range(HALF // 16):
                onehot[block * 16 : block * 16 + 16, cols] = jnp.where(
                    z == block, jnp.ones_like(z), jnp.zeros_like(z)
                )
        for g in range(BATCH):
            a = i * BATCH + g
            r16 = []
            for j in range(BASIS // 2):
                r16.append(
                    jnp.concatenate(
                        [
                            jnp.broadcast_to(r_t[2 * j + k, pl.ds(a, 1), :], (8, EDGES))
                            for k in range(2)
                        ],
                        axis=0,
                    ).astype(BF16)
                )
            for m in range(PARTS):
                y16 = jnp.where(
                    owner, jnp.broadcast_to(y_t[m, pl.ds(a, 1), :], (16, EDGES)), 0.0
                ).astype(BF16)
                for j in range(BASIS // 2):
                    row = m * 64 + j * 16
                    lhs[g, row : row + 16, :] = y16 * r16[j]
        for g in range(BATCH):
            mixed[g] = mm(lhs[g], gath[g * EDGES : (g + 1) * EDGES, :], NN)
        for g in range(BATCH):
            a = i * BATCH + g
            amps = []
            for m in range(PARTS):
                total = None
                for n in range(BASIS):
                    term = mixed[g, m * 64 + n * 8 : m * 64 + n * 8 + 8, :] * w_ref[n * 3 + DEGREE[m]]
                    total = term if total is None else total + term
                amps.append(total * norm)
            inv1 = amps[1] * amps[1] + amps[2] * amps[2] + amps[3] * amps[3]
            inv2 = sum(amps[m] * amps[m] for m in range(5, 9)) + amps[4] * amps[4]
            for l, value in enumerate((amps[0], inv1, inv2)):
                inv[l, pl.ds(a, 8, stride=LANES), :] = value
            d_l = [d_inv[l, pl.ds(a, 8, stride=LANES), :] * norm for l in range(3)]
            d_amps = [d_l[0]]
            for m in range(1, PARTS):
                d_amps.append(2.0 * amps[m] * d_l[DEGREE[m]])
            for n in range(BASIS):
                for l in range(3):
                    total = None
                    for m in range(PARTS):
                        if DEGREE[m] != l:
                            continue
                        term = mixed[g, m * 64 + n * 8 : m * 64 + n * 8 + 8, :] * d_amps[m]
                        total = term if total is None else total + term
                    rad_acc[n * 3 + l] += total
            for m in range(PARTS):
                for j in range(BASIS // 2):
                    row = m * 64 + j * 16
                    d_mix[g, row : row + 16, :] = jnp.concatenate(
                        [d_amps[m] * w_ref[(2 * j + k) * 3 + DEGREE[m]] for k in range(2)], axis=0
                    ).astype(BF16)
        for g in range(BATCH):
            a = i * BATCH + g
            cols = slice(g * EDGES, (g + 1) * EDGES)
            second = jnp.broadcast_to(half[pl.ds(a, 1), :], (C, EDGES)) > 0.5
            d_t = mm(d_mix[g], lhs[g], TN)
            back[0:C, cols] = jnp.where(second, 0.0, d_t).astype(BF16)
            back[C : 2 * C, cols] = jnp.where(second, d_t, 0.0).astype(BF16)
        for first in range(0, HALF, CHUNK):
            rows = slice(first, first + CHUNK)
            acc[rows, :] += mm(onehot[rows, :], back[...], NT)
        return carry

    lax.fori_loop(0, LANES // BATCH, step, 0)

    d_out = jnp.zeros((3 * C, C), F32)
    read_rows = [jnp.zeros((1, C), F32) for _ in range(4)]
    for q in range(PER):
        rows = slice(q * LANES, (q + 1) * LANES)
        invariants = jnp.concatenate([inv[l, rows, :] for l in range(3)], axis=1).astype(BF16)
        updated = mm(invariants, out_w[...], NN) + features[rows, :].astype(F32)
        kind = jnp.swapaxes(jnp.broadcast_to(species[q : q + 1, :], (LANES, LANES)), 0, 1)
        weight = jnp.swapaxes(jnp.broadcast_to(cot[q : q + 1, :], (LANES, LANES)), 0, 1)
        readout = jnp.zeros((LANES, C), F32)
        for t in range(4):
            readout = jnp.where(kind == t, read_w[t : t + 1, :], readout)
            read_rows[t] = read_rows[t] + jnp.sum(
                jnp.where(kind == t, weight * updated, 0.0), axis=0, keepdims=True
            )
        energy_ref[q : q + 1, :] = jnp.sum(
            jnp.swapaxes(updated * readout, 0, 1), axis=0, keepdims=True
        )
        d_rounded = d_upd_ref[rows, :].astype(BF16)
        d_out = d_out + mm(invariants, d_rounded, TN)
    d_own = acc[0:ATOMS, 0:C]
    d_own_ref[...] = d_own
    d_outer = jnp.concatenate([acc[ATOMS:HALF, 0:C], acc[:, C : 2 * C]], axis=0).astype(BF16)
    d_win_ref[...] = jnp.zeros_like(d_win_ref)
    done = 0
    for first, last in OUTER:
        count = (last - first) * 32
        d_win_ref[first * 32 : last * 32, :] = d_outer[done : done + count]
        done += count
    d_win = d_win_ref[...]
    up_sum = mm(features[...], d_own.astype(BF16), TN) + mm(window[...], d_win, TN)
    large = jnp.concatenate([up_sum, d_out], axis=0)
    blank = jnp.zeros((8, C), F32)
    for piece in range(16):
        if piece < 3:
            small = jnp.concatenate(
                [jnp.sum(rad_acc[n * 3 + piece], axis=0, keepdims=True) for n in range(BASIS)], axis=0
            )
        elif piece == 3:
            small = jnp.concatenate(read_rows + [jnp.zeros((4, C), F32)], axis=0)
        else:
            small = blank
        grads_ref[piece] = jnp.concatenate(
            [large[piece * 32 : piece * 32 + 32], small, blank], axis=0
        ).astype(BF16)


def local_terms(features, window, up, radial_w, out_w, read_w, senders, live, harm, radial, species, cot):
    vm = pl.BlockSpec(memory_space=pltpu.VMEM)
    return pl.pallas_call(
        local_kernel,
        out_shape=(
            jax.ShapeDtypeStruct((PER, LANES), F32),
            jax.ShapeDtypeStruct((ATOMS, C), F32),
            jax.ShapeDtypeStruct((ATOMS, C), F32),
            jax.ShapeDtypeStruct((WINDOW, C), BF16),
            jax.ShapeDtypeStruct((16, 48, C), BF16),
        ),
        in_specs=[vm] * 12,
        out_specs=(vm,) * 5,
        scratch_shapes=[
            pltpu.VMEM((HALF, 2 * C), BF16),
            pltpu.VMEM((LANES, EDGES), F32),
            pltpu.VMEM((LANES, EDGES), F32),
            pltpu.VMEM((LANES, EDGES), F32),
            pltpu.VMEM((LANES, EDGES), F32),
            pltpu.VMEM((LANES, EDGES), F32),
            pltpu.VMEM((PARTS, LANES, EDGES), F32),
            pltpu.VMEM((BASIS, LANES, EDGES), F32),
            pltpu.VMEM((3 * BASIS, 8, C), F32),
            pltpu.VMEM((HALF, BATCH * EDGES), BF16),
            pltpu.VMEM((BATCH, PARTS * BASIS * 8, EDGES), BF16),
            pltpu.VMEM((BATCH, PARTS * BASIS * 8, C), F32),
            pltpu.VMEM((3, ATOMS, C), F32),
            pltpu.VMEM((3, ATOMS, C), F32),
            pltpu.VMEM((HALF, 2 * C), F32),
            pltpu.VMEM((BATCH * EDGES, C), BF16),
            pltpu.VMEM((2 * C, BATCH * EDGES), BF16),
            pltpu.VMEM((BATCH, PARTS * BASIS * 8, C), BF16),
            pltpu.VMEM((3 * BASIS, 8, C), F32),
        ],
        compiler_params=pltpu.CompilerParams(vmem_limit_bytes=60 * 1024 * 1024),
    )(features, window, up, radial_w, out_w, read_w, senders, live, harm, radial, species, cot)


AXES = ("gx", "gy", "gz")
MESH = pl.DeviceIdType.MESH
GHOST = 32
PIECES = 16
PIECE_ROWS = 48


def place():
    return {axis: lax.axis_index(axis) for axis in AXES}


def shifted(axis, by):
    me = place()
    me[axis] = lax.rem(me[axis] + by + lax.axis_size(axis), lax.axis_size(axis))
    return tuple(me[name] for name in AXES)


def remote(source, target, send, arrive, device):
    return pltpu.make_async_remote_copy(
        src_ref=source,
        dst_ref=target,
        send_sem=send,
        recv_sem=arrive,
        device_id=device,
        device_id_type=MESH,
    )


def column(row):
    return jnp.swapaxes(jnp.broadcast_to(row, (LANES, LANES)), 0, 1)


def spread_kernel(features, ghost_rows, window, ghost, send, arrive):
    barrier = pltpu.get_barrier_semaphore()
    for axis in AXES:
        for by in (1, -1):
            pl.semaphore_signal(barrier, inc=1, device_id=shifted(axis, by), device_id_type=MESH)
    lane = lax.broadcasted_iota(jnp.int32, (LANES, LANES), 1)
    for h in range(2):
        row = jnp.concatenate(
            [ghost_rows[h, j, k : k + 1, :] for j in range(2) for k in range(2)], axis=1
        )
        ghost[h : h + 1, :] = row
        rows = column(row)
        hot = jnp.concatenate(
            [
                jnp.where(rows == lane + block * LANES, 1.0, 0.0).astype(BF16)
                for block in range(ATOMS // LANES)
            ],
            axis=1,
        )
        picked = mm(hot, features[...], NN).astype(BF16)
        for j in range(2):
            for k in range(2):
                first = (j * 2 + k) * GHOST
                window[1 + h, 1 + j, 1 + k] = picked[first : first + GHOST, :]
    pl.semaphore_wait(barrier, 6)
    inner = pl.ds(1, 2)
    plans = (
        ("gy", lambda at: window.at[inner, at, inner]),
        ("gx", lambda at: window.at[at, :, inner]),
        ("gz", lambda at: window.at[:, :, at]),
    )
    for number, (axis, view) in enumerate(plans):
        up = remote(
            view(2), view(0), send.at[2 * number], arrive.at[2 * number], shifted(axis, 1)
        )
        down = remote(
            view(1), view(3), send.at[2 * number + 1], arrive.at[2 * number + 1], shifted(axis, -1)
        )
        up.start()
        down.start()
        up.wait()
        down.wait()


def spread(features, ghost_rows):
    vm = pl.BlockSpec(memory_space=pltpu.VMEM)
    return pl.pallas_call(
        spread_kernel,
        out_shape=(
            jax.ShapeDtypeStruct((4, 4, 4, GHOST, C), BF16),
            jax.ShapeDtypeStruct((2, LANES), jnp.int32),
        ),
        in_specs=[vm] * 2,
        out_specs=(vm,) * 2,
        cost_estimate=pl.CostEstimate(
            flops=2 * 256 * ATOMS * C, bytes_accessed=60_000_000, transcendentals=0
        ),
        scratch_shapes=[pltpu.SemaphoreType.DMA((6,)), pltpu.SemaphoreType.DMA((6,))],
        compiler_params=pltpu.CompilerParams(
            collective_id=0, has_side_effects=True, vmem_limit_bytes=60 * 1024 * 1024
        ),
    )(features, ghost_rows)


def plane_device(by):
    return shifted("gz", by)


def stack_device(by):
    me = place()
    wide = lax.axis_size("gy")
    count = lax.axis_size("gx") * wide
    other = lax.rem(me["gx"] * wide + me["gy"] + by, count)
    return (lax.div(other, wide), lax.rem(other, wide), me["gz"]), other


def finish_kernel(
    d_win, grads, summed, returned,
    from_z, from_x, from_y, wide, narrow, first, second, third,
    near_send, near_arrive, send1, arrive1, send2, arrive2, send3, arrive3,
):
    me = place()
    k = me["gz"]
    s = me["gx"] * lax.axis_size("gy") + me["gy"]

    barrier = pltpu.get_barrier_semaphore()

    def greet(by, carry):
        pl.semaphore_signal(barrier, inc=1, device_id=plane_device(by), device_id_type=MESH)
        pl.semaphore_signal(barrier, inc=1, device_id=stack_device(by)[0], device_id_type=MESH)
        return carry

    lax.fori_loop(1, PIECES, greet, 0)
    pl.semaphore_wait(barrier, 2 * (PIECES - 1))

    def near(number, low_view, high_view, landing, axis):
        down = remote(
            low_view, landing.at[0], near_send.at[2 * number], near_arrive.at[2 * number],
            shifted(axis, -1),
        )
        above = remote(
            high_view, landing.at[1], near_send.at[2 * number + 1], near_arrive.at[2 * number + 1],
            shifted(axis, 1),
        )
        down.start()
        above.start()
        return down, above

    copies_z = near(0, d_win.at[:, :, 0], d_win.at[:, :, 3], from_z, "gz")

    def copy1(by):
        target = lax.rem(k + by, PIECES)
        return remote(
            grads.at[target], first.at[k], send1.at[target], arrive1.at[k], plane_device(by)
        )

    def copy2(by):
        device, other = stack_device(by)
        return remote(second.at[s], second.at[s], send2.at[other], arrive2.at[s], device)

    def copy3(by):
        target = lax.rem(k + by, PIECES)
        return remote(third.at[k], third.at[k], send3.at[target], arrive3.at[k], plane_device(by))

    def started(copy):
        def body(by, carry):
            copy(by).start()
            return carry

        lax.fori_loop(1, PIECES, body, 0)

    def settled(copy, slots, sems, mine):
        def body(by, carry):
            copy(by).wait_send()
            source = lax.rem(mine + by, PIECES)
            remote(
                slots.at[source], slots.at[source], sems.at[source], sems.at[source],
                plane_device(1),
            ).wait_recv()
            return carry

        lax.fori_loop(1, PIECES, body, 0)

    started(copy1)
    first[k] = grads[k]

    for copy in copies_z:
        copy.wait()
    wide[:, :, 0] = (d_win[:, :, 1].astype(F32) + from_z[1].astype(F32)).astype(BF16)
    wide[:, :, 1] = (d_win[:, :, 2].astype(F32) + from_z[0].astype(F32)).astype(BF16)
    copies_x = near(1, wide.at[0], wide.at[3], from_x, "gx")

    settled(copy1, first, arrive1, k)
    second[s] = sum_of(first)
    started(copy2)

    for copy in copies_x:
        copy.wait()
    narrow[0] = (wide[1].astype(F32) + from_x[1].astype(F32)).astype(BF16)
    narrow[1] = (wide[2].astype(F32) + from_x[0].astype(F32)).astype(BF16)
    copies_y = near(2, narrow.at[:, 0], narrow.at[:, 3], from_y, "gy")

    settled(copy2, second, arrive2, s)
    third[k] = sum_of(second)
    started(copy3)

    for copy in copies_y:
        copy.wait()
    for h in range(2):
        sides = (
            narrow[h, 1].astype(F32) + from_y[1, h].astype(F32),
            narrow[h, 2].astype(F32) + from_y[0, h].astype(F32),
        )
        for j in range(2):
            returned[h, j] = sides[j].astype(BF16)

    settled(copy3, third, arrive3, k)
    summed[...] = third[...]


def result_kernel(
    scale, third, returned, d_own, d_upd, ghost, up,
    feature_grad, up_grad, rad_grad, out_grad, read_grad,
):
    atom = lax.broadcasted_iota(jnp.int32, (ATOMS, LANES), 0)
    total = d_own[...]
    for h in range(2):
        hot = jnp.where(atom == ghost[h : h + 1, :], 1.0, 0.0).astype(BF16)
        total = total + mm(hot, returned[h * LANES : (h + 1) * LANES, :], NN)
    feature_grad[...] = mm(total.astype(BF16), up[...], NT) + d_upd[...]
    for piece in range(4):
        up_grad[piece * 32 : piece * 32 + 32, :] = third[piece, 0:32].astype(F32) * scale
    for piece in range(12):
        out_grad[piece * 32 : piece * 32 + 32, :] = third[4 + piece, 0:32].astype(F32) * scale
    for l in range(3):
        rad_grad[:, l * C : (l + 1) * C] = third[l, 32:48].astype(F32)[0:8] * scale
    read_grad[...] = third[3, 32:48].astype(F32)[0:4] * scale


def result(scale, *operands):
    vm = pl.BlockSpec(memory_space=pltpu.VMEM)
    return pl.pallas_call(
        functools.partial(result_kernel, scale),
        out_shape=(
            jax.ShapeDtypeStruct((ATOMS, C), F32),
            jax.ShapeDtypeStruct((C, C), F32),
            jax.ShapeDtypeStruct((BASIS, 3 * C), F32),
            jax.ShapeDtypeStruct((3 * C, C), F32),
            jax.ShapeDtypeStruct((4, C), F32),
        ),
        in_specs=[vm] * len(operands),
        out_specs=(vm,) * 5,
        compiler_params=pltpu.CompilerParams(vmem_limit_bytes=60 * 1024 * 1024),
    )(*operands)


def sum_of(slots):
    total = slots[0].astype(F32)
    for piece in range(1, PIECES):
        total = total + slots[piece].astype(F32)
    return total.astype(BF16)


def finish(d_win, grads):
    vm = pl.BlockSpec(memory_space=pltpu.VMEM)
    sems = pltpu.SemaphoreType.DMA((PIECES,))
    return pl.pallas_call(
        finish_kernel,
        out_shape=(
            jax.ShapeDtypeStruct((PIECES, PIECE_ROWS, C), BF16),
            jax.ShapeDtypeStruct((2, 2, 2, GHOST, C), BF16),
        ),
        in_specs=[vm] * 2,
        out_specs=(vm,) * 2,
        scratch_shapes=[
            pltpu.VMEM((2, 4, 4, GHOST, C), BF16),
            pltpu.VMEM((2, 4, 2, GHOST, C), BF16),
            pltpu.VMEM((2, 2, 2, GHOST, C), BF16),
            pltpu.VMEM((4, 4, 2, GHOST, C), BF16),
            pltpu.VMEM((2, 4, 2, GHOST, C), BF16),
            pltpu.VMEM((PIECES, PIECE_ROWS, C), BF16),
            pltpu.VMEM((PIECES, PIECE_ROWS, C), BF16),
            pltpu.VMEM((PIECES, PIECE_ROWS, C), BF16),
            pltpu.SemaphoreType.DMA((6,)),
            pltpu.SemaphoreType.DMA((6,)),
            sems, sems, sems, sems, sems, sems,
        ],
        compiler_params=pltpu.CompilerParams(
            collective_id=1, has_side_effects=True, vmem_limit_bytes=60 * 1024 * 1024
        ),
    )(d_win, grads)


def per_device(
    features, up_weight, radial_weight, out_weight, read_weight,
    ghost_rows, senders, live, harmonics, radial, species, cotangent,
):
    window, ghost = spread(features, ghost_rows)
    energy, d_upd, d_own, d_win, grads = local_terms(
        features, window.reshape(WINDOW, C), up_weight, radial_weight, out_weight, read_weight,
        senders, live, harmonics, radial,
        species.reshape(PER, LANES), cotangent.reshape(PER, LANES),
    )
    scale = 1.0 / math.sqrt(ATOMS * lax.axis_size("gx") * lax.axis_size("gy") * lax.axis_size("gz"))
    summed, returned = finish(d_win.reshape(4, 4, 4, GHOST, C), grads)
    feature_grad, up_grad, rad_grad, out_grad, read_grad = result(
        scale, summed, returned.reshape(2 * LANES, C), d_own, d_upd, ghost, up_weight
    )
    return energy.reshape(ATOMS), feature_grad, up_grad, rad_grad, out_grad, read_grad


def solution(mesh):
    whole = P(AXES)
    in_specs = (
        P(AXES, None), P(), P(), P(), P(),
        P("gx", "gy", "gz", None), P(None, AXES), P(None, AXES), P(None, None, AXES),
        P(None, None, AXES), whole, whole,
    )
    out_specs = (whole, P(AXES, None), P(), P(), P(), P())
    return jax.shard_map(
        per_device, mesh=mesh, in_specs=in_specs, out_specs=out_specs, check_vma=False
    )
```
